256 devices in a mesh: dp: 16 (over z, y_hi), seq: 16 (over y_lo, x, core).
Axes of the slice: x: 4, y: 4 (y_hi: 2, y_lo: 2; y = y_hi * 2 + y_lo), z: 8, core: 2. Of those that a mesh axis runs over, the one named last changes fastest.
Arguments:
- frames: bfloat16 [16, 4096, 1536], P('dp', 'seq'), may hold values from -6 to 6
- arrival: int32 [16, 16], replicated, may hold values from 0 to 15, as said below
- lengths: int32 [16], replicated, may hold values from 1024 to 4096, as said below
- attn_gain: float32 [1536], replicated, may hold values from 0.1 to 1.9
- w_qkv: bfloat16 [1536, 4608], P('dp'), may hold values from -8 to 8
- w_out: bfloat16 [1536, 1536], replicated, may hold values from -0.15625 to 0.15625
- conv_gain: float32 [1536], replicated, may hold values from 0.1 to 1.9
- conv_kernel: float32 [31, 1536], replicated, may hold values from -2 to 2
Outputs:
- encoded: bfloat16 [16, 4096, 1536], P('dp', 'seq')
The draws below stay inside these ranges and needn't reach their ends.
Inputs may be any that keep to these rules, and one draw needn't show every extreme that they name: arrival[s] is a permutation of the 16 data groups for every s. `lengths`: at least one recording fills its whole slot.
All inputs are finite; a program needn't handle non-finite values.
Results may differ from the reference program's by a relative error of at most 0.0085.
Values may be sent and summed in bfloat16 or wider, within the bound.
No kernel may reach another device: no remote copies, remote signals or barrier semaphores. Data moves between devices by JAX's collectives and lax.ppermute only.
A program may use at most 128 MiB of HBM per device.

```python
import jax
import jax.numpy as jnp
from jax import lax

D = 1536
HEAD = 64
HD = 1536
C = 256
KERNEL = 31
ITERS = 2
FRAMES = 4096
RECS = 16
N_DP = 16
N_SEQ = 16


def draw_arrival(key, part):
    key = jax.random.fold_in(key, 2)
    keys = jax.random.split(key, N_SEQ)
    return jax.vmap(lambda k: jax.random.permutation(k, N_DP))(keys).astype(jnp.int32)


def draw_lengths(key, part):
    key = jax.random.fold_in(key, 1)
    spread = jax.random.randint(key, (N_DP,), FRAMES // 4, FRAMES + 1)
    chosen = jax.random.randint(jax.random.fold_in(key, 5), (), 0, N_DP)
    return jnp.where(jnp.arange(N_DP) == chosen, FRAMES, spread).astype(jnp.int32)


def draw_frames(key, part):
    key = jax.random.fold_in(key, 3)
    base = jax.random.normal(key, (RECS, FRAMES, D), jnp.float32)
    return jnp.clip(base, -6.0, 6.0).astype(jnp.bfloat16)


def draw_w_qkv(key, part):
    key = jax.random.fold_in(key, 4)
    base = jnp.clip(jax.random.normal(key, (D, 3 * HD), jnp.float32), -6.0, 6.0) * D ** (-0.5)
    return base.astype(jnp.bfloat16)


def gaussian(key, extent, deviation, limit, kind=jnp.bfloat16):
    values = jax.random.normal(key, extent, jnp.float32) * deviation
    return jnp.minimum(jnp.maximum(values, -limit), limit).astype(kind)


def setup_inputs(seed: int = 0) -> dict:
    key_of = jax.random.split(jax.random.key(seed), 9)
    return {
        "frames": draw_frames(jax.random.fold_in(key_of[8], 71), 0),
        "arrival": draw_arrival(jax.random.fold_in(key_of[8], 71), 0),
        "lengths": draw_lengths(jax.random.fold_in(key_of[8], 71), 0),
        "attn_gain": jnp.clip(1.0 + 0.18 * jax.random.normal(key_of[3], (D,), jnp.float32), 0.1, 1.9),
        "w_qkv": draw_w_qkv(jax.random.fold_in(key_of[8], 71), 0),
        "w_out": gaussian(key_of[5], (HD, D), HD ** -0.5, 0.15625),
        "conv_gain": jnp.clip(1.0 + 0.18 * jax.random.normal(key_of[6], (D,), jnp.float32), 0.1, 1.9),
        "conv_kernel": gaussian(key_of[7], (KERNEL, D), (KERNEL // 4) ** -0.5, 2.0, jnp.float32),
    }


def norm(v):
    mean = lax.optimization_barrier(jnp.mean(v, axis=-1, keepdims=True))
    var = lax.optimization_barrier(jnp.mean((v - mean) ** 2, axis=-1, keepdims=True))
    return (v - mean) / jnp.sqrt(var + 1e-05)

def one_recording(args, attn_gain, w_qkv, w_out, conv_gain, conv_kernel):
    x, length = args
    total = x.shape[0]
    spans = total // C
    width = w_out.shape[0]
    heads = width // HEAD
    position = jnp.arange(total)
    valid = (position < length).astype(jnp.float32)
    own_valid = (position < length).reshape(spans, C)
    left_valid = jnp.concatenate([jnp.zeros((1, C), bool), own_valid[:-1]], axis=0)
    key_valid = jnp.concatenate([left_valid, own_valid], axis=1)
    half = (KERNEL - 1) // 2
    for step in range(ITERS):
        h = (norm(x.astype(jnp.float32)) * attn_gain).astype(jnp.bfloat16)
        qkv = jnp.dot(h, w_qkv, preferred_element_type=jnp.float32).astype(jnp.bfloat16)
        query = qkv[:, :width].reshape(spans, C, heads, HEAD)
        keys = qkv[:, width:2 * width].reshape(spans, C, heads, HEAD)
        values = qkv[:, 2 * width:].reshape(spans, C, heads, HEAD)
        zero_span = jnp.zeros((1, C, heads, HEAD), jnp.bfloat16)
        keys = jnp.concatenate([jnp.concatenate([zero_span, keys[:-1]], 0), keys], axis=1)
        values = jnp.concatenate([jnp.concatenate([zero_span, values[:-1]], 0), values], axis=1)
        scores = jnp.einsum('schd,skhd->shck', query.astype(jnp.float32), keys.astype(jnp.float32)) * HEAD ** (-0.5)
        scores = jnp.where(key_valid[:, None, None, :], scores, -1e+30)
        top = lax.optimization_barrier(jnp.max(scores, axis=-1, keepdims=True))
        expo = jnp.exp(scores - top)
        probs = (expo / lax.optimization_barrier(jnp.sum(expo, axis=-1, keepdims=True))).astype(jnp.bfloat16)
        ctx = jnp.einsum('shck,skhd->schd', probs.astype(jnp.float32), values.astype(jnp.float32))
        ctx = ctx.astype(jnp.bfloat16).reshape(total, width)
        x1 = x.astype(jnp.float32) + jnp.dot(ctx, w_out, preferred_element_type=jnp.float32)
        g = (norm(x1) * conv_gain * valid[:, None]).astype(jnp.bfloat16)
        padded = jnp.pad(g.astype(jnp.float32), ((half, half), (0, 0)))
        conv = jnp.zeros_like(x1)
        for tap in range(KERNEL):
            conv = conv + conv_kernel[tap] * padded[tap:tap + total]
        x = ((x1 + jax.nn.silu(conv)) * valid[:, None]).astype(jnp.bfloat16)
    return x

def reference(frames, arrival, lengths, attn_gain, w_qkv, w_out, conv_gain, conv_kernel):
    recs, total, width = frames.shape
    spans = total // C
    blocks = frames.reshape(recs, spans, C, width)
    ordered = blocks[arrival.T, jnp.arange(spans)[None, :]].reshape(recs, total, width)
    return lax.map(lambda a: one_recording(a, attn_gain, w_qkv, w_out, conv_gain, conv_kernel), (ordered, lengths))
```

```python
import functools

import jax
import jax.numpy as jnp
from jax import lax
from jax.experimental import pallas as pl
from jax.experimental.pallas import tpu as pltpu
from jax.sharding import Mesh, PartitionSpec as P

HEAD = 64
KERNEL = 31
ITERS = 2
HALO = 16
EPS = 1e-05
DP = ("z", "yh")
SEQ = ("yl", "x", "core")
BF = jnp.bfloat16
F32 = jnp.float32
VMEM = 48 * 1024 * 1024


def params(**kw):
    return pltpu.CompilerParams(vmem_limit_bytes=VMEM, **kw)


def normed(v):
    mean = jnp.mean(v, axis=-1, keepdims=True)
    d = v - mean
    var = jnp.mean(d * d, axis=-1, keepdims=True)
    return d * lax.rsqrt(var + EPS)


def pick_kernel(row_ref, in_ref, out_ref):
    for r in range(in_ref.shape[0]):
        out_ref[r] = in_ref[row_ref[r]]


def pick(chunks, row):
    return pl.pallas_call(
        pick_kernel,
        out_shape=jax.ShapeDtypeStruct(chunks.shape, chunks.dtype),
        in_specs=[
            pl.BlockSpec(memory_space=pltpu.SMEM),
            pl.BlockSpec(memory_space=pltpu.VMEM),
        ],
        out_specs=pl.BlockSpec(memory_space=pltpu.VMEM),
        compiler_params=params(),
        name="pick",
    )(row, chunks)


def head_kernel(x_ref, gain_ref, perm_ref, out_ref):
    h = (normed(x_ref[...].astype(F32)) * gain_ref[...]).astype(BF)
    out_ref[...] = jnp.dot(h, perm_ref[...], preferred_element_type=F32).astype(BF)


def head(x, gain, perm):
    return pl.pallas_call(
        head_kernel,
        out_shape=jax.ShapeDtypeStruct(x.shape, BF),
        compiler_params=params(),
        name="head",
    )(x, gain, perm)


def project_kernel(h_ref, w_ref, out_ref):
    depth = w_ref.shape[0] * w_ref.shape[2]
    w = w_ref[...].reshape(depth, w_ref.shape[3])
    out_ref[0] = jnp.dot(h_ref[...], w, preferred_element_type=F32).astype(BF)


def project(h, w):
    parts, blocks, rows, cols = w.shape
    span, width = h.shape
    return pl.pallas_call(
        project_kernel,
        grid=(blocks,),
        out_shape=jax.ShapeDtypeStruct((blocks, span, cols), BF),
        in_specs=[
            pl.BlockSpec((span, width), lambda b: (0, 0)),
            pl.BlockSpec((parts, 1, rows, cols), lambda b: (0, b, 0, 0)),
        ],
        out_specs=pl.BlockSpec((1, span, cols), lambda b: (b, 0, 0)),
        compiler_params=params(),
        name="project",
    )(h, w)


def attend_kernel(
    left_ref, own_ref, w_ref, wout_ref, x_ref, bias_ref, gain_ref, valid_ref,
    x1_ref, g_ref, acc_ref,
):
    b = pl.program_id(0)
    span = left_ref.shape[0]
    group = wout_ref.shape[0]
    w = w_ref[...].reshape(w_ref.shape[0] * w_ref.shape[2], w_ref.shape[3])
    kv_left = jnp.dot(left_ref[...], w, preferred_element_type=F32).astype(BF)
    lane = lax.broadcasted_iota(jnp.int32, (span, 128), 1)
    low = lane < HEAD
    tag = jnp.where(lane == 0, 1.0, 0.0).astype(BF)
    ones = jnp.ones((2 * span, 128), BF)
    outs = []
    for p in range(group // 128):
        at = 128 * p
        k = jnp.concatenate([kv_left[:, at : at + 128], own_ref[0, :, at : at + 128]], axis=0)
        k = jnp.concatenate([k, bias_ref[...]], axis=1)
        at = group + 128 * p
        v = jnp.concatenate([kv_left[:, at : at + 128], own_ref[0, :, at : at + 128]], axis=0)
        v = jnp.concatenate([v, ones], axis=1)
        at = 2 * group + 128 * p
        q = own_ref[0, :, at : at + 128] * jnp.asarray(HEAD ** (-0.5), BF)
        halves = []
        for mask in (low, jnp.logical_not(low)):
            qh = jnp.where(mask, q, jnp.zeros_like(q))
            qh = jnp.concatenate([qh, tag], axis=1)
            s = lax.dot_general(qh, k, (((1,), (1,)), ((), ())), preferred_element_type=F32)
            top = jnp.max(s, axis=-1, keepdims=True)
            e = jnp.exp(s - top).astype(BF)
            o = jnp.dot(e, v, preferred_element_type=F32)
            halves.append(o[:, :128] / o[:, 128:])
        outs.append(jnp.where(low, halves[0], halves[1]).astype(BF))
    ctx = jnp.concatenate(outs, axis=1)
    part = jnp.dot(ctx, wout_ref[...], preferred_element_type=F32)

    @pl.when(b == 0)
    def _():
        acc_ref[...] = part

    @pl.when(b > 0)
    def _():
        acc_ref[...] += part

    @pl.when(b == pl.num_programs(0) - 1)
    def _():
        x1 = x_ref[...].astype(F32) + acc_ref[...]
        x1_ref[...] = x1
        g_ref[...] = (normed(x1) * gain_ref[...] * valid_ref[...]).astype(BF)


def attend(left, own, w, w_out, x, bias, gain, valid):
    parts, blocks, rows, cols = w.shape
    span, width = x.shape
    group = width // blocks
    whole = lambda *shape: pl.BlockSpec(shape, lambda b: (0,) * len(shape))
    return pl.pallas_call(
        attend_kernel,
        grid=(blocks,),
        out_shape=(
            jax.ShapeDtypeStruct((span, width), F32),
            jax.ShapeDtypeStruct((span, width), BF),
        ),
        in_specs=[
            whole(span, width),
            pl.BlockSpec((1, span, cols), lambda b: (b, 0, 0)),
            pl.BlockSpec((parts, 1, rows, 2 * group), lambda b: (0, b, 0, 0)),
            pl.BlockSpec((group, width), lambda b: (b, 0)),
            whole(span, width),
            whole(2 * span, 128),
            whole(1, width),
            whole(span, 1),
        ],
        out_specs=(whole(span, width), whole(span, width)),
        scratch_shapes=[pltpu.VMEM((span, width), F32)],
        compiler_params=params(),
        name="attend",
    )(left, own, w, w_out, x, bias, gain, valid)


def conv_kernel_body(last, g_ref, low_ref, high_ref, x1_ref, taps_ref, valid_ref, *rest):
    if last:
        x_ref, pad_ref = rest
    else:
        gain_ref, perm_ref, x_ref, h_ref, pad_ref = rest
    span, width = x1_ref.shape
    valid = valid_ref[...]
    for c in range(width // 128):
        cols = pl.ds(128 * c, 128)
        pad_ref[pl.ds(0, HALO), :] = low_ref[:, cols].astype(F32)
        pad_ref[pl.ds(HALO, span), :] = g_ref[:, cols].astype(F32)
        pad_ref[pl.ds(HALO + span, HALO), :] = high_ref[:, cols].astype(F32)
        taps = taps_ref[:, cols]
        y = jnp.zeros((span, 128), F32)
        for r in range(8):
            hits = [(j, (j + 1) // 8) for j in range(KERNEL) if (j + 1) % 8 == r]
            deep = max(m for _, m in hits)
            moved = pad_ref[pl.ds(r, span + 8 * deep), :]
            for j, m in hits:
                y = y + taps[j : j + 1, :] * moved[8 * m : 8 * m + span]
        silu = y / (1.0 + jnp.exp(-y))
        x_ref[:, cols] = ((x1_ref[:, cols] + silu) * valid).astype(BF)
    if not last:
        h = (normed(x_ref[...].astype(F32)) * gain_ref[...]).astype(BF)
        h_ref[...] = jnp.dot(h, perm_ref[...], preferred_element_type=F32).astype(BF)


def convolve(g, low, high, x1, taps, valid, gain, perm, last):
    span, width = x1.shape
    out = [jax.ShapeDtypeStruct((span, width), BF)]
    args = [g, low, high, x1, taps, valid]
    if not last:
        out.append(out[0])
        args += [gain, perm]
    return pl.pallas_call(
        functools.partial(conv_kernel_body, last),
        out_shape=tuple(out),
        scratch_shapes=[pltpu.VMEM((span + 2 * HALO, 128), F32)],
        compiler_params=params(),
        name="convolve",
    )(*args)


def along(value, by):
    size = lax.axis_size(SEQ)
    pairs = [(i, i + by) for i in range(size) if 0 <= i + by < size]
    return lax.ppermute(value, SEQ, pairs)


def weight_blocks(w, frames):
    rows, cols = w.shape
    zs, xs = lax.axis_size("z"), lax.axis_size("x")
    deep = rows // (lax.axis_size("yl") * lax.axis_size("core"))
    width = cols // 3
    group = width // xs
    at = (lax.axis_index("yl") * lax.axis_size("core") + lax.axis_index("core")) * deep
    col = lax.axis_index("x") * group
    own = jnp.concatenate(
        [lax.dynamic_slice(w, (at, part * width + col), (deep, group)) for part in (1, 2, 0)],
        axis=1,
    )
    pieces = {0: own}
    for step in range(1, zs // 2 + 1):
        for k in {step, zs - step}:
            pieces[k] = lax.ppermute(own, "z", [(i, (i + k) % zs) for i in range(zs)])
    stack = jnp.concatenate([pieces[k] for k in range(zs)], axis=0)
    stack, frames = lax.optimization_barrier((stack, frames))
    full = lax.all_gather(stack, ("yh",) + SEQ, axis=0, tiled=True)
    parts = lax.axis_size("yh") * lax.axis_size("yl")
    return full.reshape(parts, xs, -1, 3 * group), frames


def order(width, deep):
    zs = lax.axis_size("z")
    cores = lax.axis_size("core")
    yls = lax.axis_size("yl")
    place = jnp.arange(width)
    i = place % deep
    k = place // deep % zs
    core = place // (deep * zs) % cores
    yl = place // (deep * zs * cores) % yls
    yh = place // (deep * zs * cores * yls)
    z = (lax.axis_index("z") - k) % zs
    feature = (z * lax.axis_size("yh") + yh) * (yls * cores * deep) + (yl * cores + core) * deep + i
    return (jnp.arange(width)[:, None] == feature[None, :]).astype(BF)


def on_device(frames, arrival, lengths, attn_gain, w_qkv, w_out, conv_gain, conv_kernel):
    span = frames.shape[1]
    width = w_out.shape[0]
    group = lax.axis_index(DP)
    place = lax.axis_index(SEQ)
    groups = lax.axis_size(DP)
    w, frames = weight_blocks(w_qkv, frames)
    row_here = lax.dynamic_index_in_dim(arrival, place, 0, keepdims=False)
    chunks = frames.reshape(groups, span // groups, width)
    chunks = lax.all_to_all(chunks, DP, split_axis=0, concat_axis=0, tiled=True)
    chunks = pick(chunks, row_here)
    chunks = lax.all_to_all(chunks, DP, split_axis=0, concat_axis=0, tiled=True)
    x = chunks.reshape(span, width)

    perm = order(width, w_qkv.shape[0] // (lax.axis_size("yl") * lax.axis_size("core")))
    length = lax.dynamic_index_in_dim(lengths, group, 0, keepdims=False)
    position = place * span + jnp.arange(span)
    own_valid = position < length
    left_valid = jnp.logical_and(position - span < length, place > 0)
    key_valid = jnp.concatenate([left_valid, own_valid])
    bias = jnp.where(key_valid, 0.0, -1e30).astype(BF)
    bias = jnp.where(jnp.arange(128)[None, :] == 0, bias[:, None], jnp.zeros((), BF))
    valid = own_valid.astype(F32)[:, None]
    gain_a = attn_gain[None, :]
    gain_c = conv_gain[None, :]
    taps = jnp.pad(conv_kernel, ((0, 1), (0, 0)))

    h = head(x, gain_a, perm)
    for step in range(ITERS):
        last = step == ITERS - 1
        left = along(h, 1)
        own = project(h, w)
        x1, g = attend(left, own, w, w_out, x, bias, gain_c, valid)
        low = along(g[span - HALO :], 1)
        high = along(g[:HALO], -1)
        out = convolve(g, low, high, x1, taps, valid, gain_a, perm, last)
        x = out[0]
        if not last:
            h = out[1]
    return x[None]


def solution(mesh):
    fine = Mesh(mesh.devices.reshape(8, 2, 2, 4, 2), DP + SEQ)
    placed = (P(DP, SEQ, None), P(), P(), P(), P(DP, None), P(), P(), P())
    return jax.shard_map(
        on_device, mesh=fine, in_specs=placed, out_specs=P(DP, SEQ, None), check_vma=False
    )
```

```python
import functools

import jax
import jax.numpy as jnp
from jax import lax
from jax.experimental import pallas as pl
from jax.experimental.pallas import tpu as pltpu
from jax.sharding import Mesh, PartitionSpec as P

HEAD = 64
KERNEL = 31
ITERS = 2
HALO = 16
EPS = 1e-05
DP = ("z", "yh")
SEQ = ("yl", "x", "core")
BF = jnp.bfloat16
F32 = jnp.float32
VMEM = 24 * 1024 * 1024


def params(**kw):
    return pltpu.CompilerParams(vmem_limit_bytes=VMEM, **kw)


def normed(v):
    mean = jnp.mean(v, axis=-1, keepdims=True)
    d = v - mean
    var = jnp.mean(d * d, axis=-1, keepdims=True)
    return d * lax.rsqrt(var + EPS)


def pick_kernel(row_ref, in_ref, out_ref):
    for r in range(in_ref.shape[0]):
        out_ref[r] = in_ref[row_ref[r]]


def pick(chunks, row):
    return pl.pallas_call(
        pick_kernel,
        out_shape=jax.ShapeDtypeStruct(chunks.shape, chunks.dtype),
        in_specs=[
            pl.BlockSpec(memory_space=pltpu.SMEM),
            pl.BlockSpec(memory_space=pltpu.VMEM),
        ],
        out_specs=pl.BlockSpec(memory_space=pltpu.VMEM),
        compiler_params=params(),
        name="pick",
    )(row, chunks)


def head_kernel(x_ref, gain_ref, out_ref):
    out_ref[...] = (normed(x_ref[...].astype(F32)) * gain_ref[...]).astype(BF)


def head(x, gain):
    return pl.pallas_call(
        head_kernel,
        out_shape=jax.ShapeDtypeStruct(x.shape, BF),
        compiler_params=params(),
        name="head",
    )(x, gain)


def project_kernel(h_ref, w_ref, out_ref):
    out_ref[0] = jnp.dot(h_ref[...], w_ref[0], preferred_element_type=F32).astype(BF)


def project(h, w):
    blocks, depth, cols = w.shape
    span, width = h.shape
    return pl.pallas_call(
        project_kernel,
        grid=(blocks,),
        out_shape=jax.ShapeDtypeStruct((blocks, span, cols), BF),
        in_specs=[
            pl.BlockSpec((span, width), lambda b: (0, 0)),
            pl.BlockSpec((1, depth, cols), lambda b: (b, 0, 0)),
        ],
        out_specs=pl.BlockSpec((1, span, cols), lambda b: (b, 0, 0)),
        compiler_params=params(),
        name="project",
    )(h, w)


def heads(query, keys, values, bias):
    span = query.shape[0]
    lane = lax.broadcasted_iota(jnp.int32, (span, 128), 1)
    low = lane < HEAD
    tag = jnp.where(lane == 0, 1.0, 0.0).astype(BF)
    ones = jnp.ones((2 * span, 128), BF)
    outs = []
    for at in range(0, query.shape[1], 128):
        k = jnp.concatenate([keys[:, at : at + 128], bias], axis=1)
        v = jnp.concatenate([values[:, at : at + 128], ones], axis=1)
        q = query[:, at : at + 128] * jnp.asarray(HEAD ** (-0.5), BF)
        halves = []
        for mask in (low, jnp.logical_not(low)):
            qh = jnp.concatenate([jnp.where(mask, q, jnp.zeros_like(q)), tag], axis=1)
            s = lax.dot_general(qh, k, (((1,), (1,)), ((), ())), preferred_element_type=F32)
            top = jnp.max(s, axis=-1, keepdims=True)
            e = jnp.exp(s - top).astype(BF)
            o = jnp.dot(e, v, preferred_element_type=F32)
            halves.append(o[:, :128] / o[:, 128:])
        outs.append(jnp.where(low, halves[0], halves[1]).astype(BF))
    return jnp.concatenate(outs, axis=1)


def settle(ctx, wout_ref, x_ref, gain_ref, valid_ref, x1_ref, g_ref, acc_ref):
    b = pl.program_id(0)
    part = jnp.dot(ctx, wout_ref[...], preferred_element_type=F32)

    @pl.when(b == 0)
    def _():
        acc_ref[...] = x_ref[...].astype(F32) + part

    @pl.when(b > 0)
    def _():
        acc_ref[...] += part

    @pl.when(b == pl.num_programs(0) - 1)
    def _():
        x1 = acc_ref[...]
        x1_ref[...] = x1
        g_ref[...] = (normed(x1) * gain_ref[...] * valid_ref[...]).astype(BF)


def opening_kernel(
    z_ref, left_ref, h_ref, w_ref, wout_ref, x_ref, bias_ref, gain_ref, valid_ref,
    x1_ref, g_ref, wall_ref, acc_ref, both_ref, buf_ref, in_sem, out_sem,
):
    b = pl.program_id(0)
    last = pl.num_programs(0) - 1
    slot = lax.rem(b, 2)
    span = h_ref.shape[0]
    group = wout_ref.shape[0]
    parts, _, zs, rows, _ = w_ref.shape

    def fetch(block, to):
        for part in range(parts):
            for z in range(zs):
                at = (z * parts + part) * rows
                pltpu.make_async_copy(
                    w_ref.at[part, block, lax.rem(z_ref[0] - z + zs, zs)],
                    buf_ref.at[to, pl.ds(at, rows)],
                    in_sem.at[to],
                ).start()

    def saved(block, at):
        return pltpu.make_async_copy(buf_ref.at[at], wall_ref.at[block], out_sem.at[at])

    @pl.when(b == 0)
    def _():
        fetch(0, 0)
        both_ref[pl.ds(0, span), :] = left_ref[...]
        both_ref[pl.ds(span, span), :] = h_ref[...]

    @pl.when(b > 0)
    def _():
        saved(b - 1, 1 - slot).wait()

    @pl.when(b < last)
    def _():
        fetch(b + 1, 1 - slot)

    pltpu.make_async_copy(wall_ref.at[b], buf_ref.at[slot], in_sem.at[slot]).wait()
    saved(b, slot).start()
    kv = jnp.dot(both_ref[...], buf_ref[slot, :, : 2 * group], preferred_element_type=F32).astype(BF)
    q = jnp.dot(h_ref[...], buf_ref[slot, :, 2 * group :], preferred_element_type=F32).astype(BF)
    ctx = heads(q, kv[:, :group], kv[:, group:], bias_ref[...])
    settle(ctx, wout_ref, x_ref, gain_ref, valid_ref, x1_ref, g_ref, acc_ref)

    @pl.when(b == last)
    def _():
        saved(b, slot).wait()


def whole(*shape):
    return pl.BlockSpec(shape, lambda b: (0,) * len(shape))


def opening(z, left, h, w, w_out, x, bias, gain, valid):
    parts, blocks, zs, rows, cols = w.shape
    span, width = x.shape
    group = width // blocks
    depth = parts * zs * rows
    return pl.pallas_call(
        opening_kernel,
        grid=(blocks,),
        out_shape=(
            jax.ShapeDtypeStruct((span, width), F32),
            jax.ShapeDtypeStruct((span, width), BF),
            jax.ShapeDtypeStruct((blocks, depth, cols), BF),
        ),
        in_specs=[
            pl.BlockSpec(memory_space=pltpu.SMEM),
            whole(span, width),
            whole(span, width),
            pl.BlockSpec(memory_space=pl.ANY),
            pl.BlockSpec((group, width), lambda b: (b, 0)),
            whole(span, width),
            whole(2 * span, 128),
            whole(1, width),
            whole(span, 1),
        ],
        out_specs=(whole(span, width), whole(span, width), pl.BlockSpec(memory_space=pl.ANY)),
        scratch_shapes=[
            pltpu.VMEM((span, width), F32),
            pltpu.VMEM((2 * span, width), BF),
            pltpu.VMEM((2, depth, cols), BF),
            pltpu.SemaphoreType.DMA((2,)),
            pltpu.SemaphoreType.DMA((2,)),
        ],
        compiler_params=params(),
        name="opening",
    )(z, left, h, w, w_out, x, bias, gain, valid)


def attend_kernel(
    left_ref, own_ref, w_ref, wout_ref, x_ref, bias_ref, gain_ref, valid_ref,
    x1_ref, g_ref, acc_ref,
):
    b = pl.program_id(0)
    group = wout_ref.shape[0]
    left = jnp.dot(left_ref[...], w_ref[0], preferred_element_type=F32).astype(BF)
    own = own_ref[b]
    keys = jnp.concatenate([left[:, :group], own[:, :group]], axis=0)
    values = jnp.concatenate([left[:, group:], own[:, group : 2 * group]], axis=0)
    ctx = heads(own[:, 2 * group :], keys, values, bias_ref[...])
    settle(ctx, wout_ref, x_ref, gain_ref, valid_ref, x1_ref, g_ref, acc_ref)


def attend(left, own, w, w_out, x, bias, gain, valid):
    blocks, depth, cols = w.shape
    span, width = x.shape
    group = width // blocks
    return pl.pallas_call(
        attend_kernel,
        grid=(blocks,),
        out_shape=(
            jax.ShapeDtypeStruct((span, width), F32),
            jax.ShapeDtypeStruct((span, width), BF),
        ),
        in_specs=[
            whole(span, width),
            pl.BlockSpec(memory_space=pltpu.VMEM),
            pl.BlockSpec((1, depth, 2 * group), lambda b: (b, 0, 0)),
            pl.BlockSpec((group, width), lambda b: (b, 0)),
            whole(span, width),
            whole(2 * span, 128),
            whole(1, width),
            whole(span, 1),
        ],
        out_specs=(whole(span, width), whole(span, width)),
        scratch_shapes=[pltpu.VMEM((span, width), F32)],
        compiler_params=params(),
        name="attend",
    )(left, own, w, w_out, x, bias, gain, valid)


def taps_over(pad_ref, taps, rows):
    y = jnp.zeros((rows, 128), F32)
    for r in range(8):
        hits = [(j, (j + 1) // 8) for j in range(KERNEL) if (j + 1) % 8 == r]
        deep = max(m for _, m in hits)
        moved = pad_ref[pl.ds(r, rows + 8 * deep), :]
        for j, m in hits:
            y = y + taps[j : j + 1, :] * moved[8 * m : 8 * m + rows]
    return y / (1.0 + jnp.exp(-y))


def inner_kernel(g_ref, x1_ref, taps_ref, valid_ref, gain_ref, x_ref, *rest):
    pad_ref = rest[-1]
    span, width = x1_ref.shape
    rows = pl.ds(HALO, span - 2 * HALO)
    for c in range(width // 128):
        cols = pl.ds(128 * c, 128)
        pad_ref[...] = g_ref[:, cols].astype(F32)
        silu = taps_over(pad_ref, taps_ref[:, cols], span - 2 * HALO)
        x_ref[rows, cols] = ((x1_ref[rows, cols] + silu) * valid_ref[rows, :]).astype(BF)
    if len(rest) > 1:
        rest[0][rows, :] = (normed(x_ref[rows, :].astype(F32)) * gain_ref[...]).astype(BF)


def inner(g, x1, taps, valid, gain, last):
    span, width = x1.shape
    return pl.pallas_call(
        inner_kernel,
        out_shape=(jax.ShapeDtypeStruct((span, width), BF),) * (1 if last else 2),
        scratch_shapes=[pltpu.VMEM((span, 128), F32)],
        compiler_params=params(),
        name="inner",
    )(g, x1, taps, valid, gain)


def edges_kernel(count, g_ref, low_ref, high_ref, x1_ref, taps_ref, valid_ref, gain_ref, *rest):
    ins, outs, pad_ref = rest[:count], rest[count:-1], rest[-1]
    span, width = x1_ref.shape
    x_ref = outs[0]
    for at in (0, span - HALO):
        rows = pl.ds(at, HALO)
        for c in range(width // 128):
            cols = pl.ds(128 * c, 128)
            if at == 0:
                pad_ref[pl.ds(0, HALO), :] = low_ref[:, cols].astype(F32)
                pad_ref[pl.ds(HALO, 2 * HALO), :] = g_ref[pl.ds(0, 2 * HALO), cols].astype(F32)
            else:
                pad_ref[pl.ds(0, 2 * HALO), :] = g_ref[pl.ds(span - 2 * HALO, 2 * HALO), cols].astype(F32)
                pad_ref[pl.ds(2 * HALO, HALO), :] = high_ref[:, cols].astype(F32)
            silu = taps_over(pad_ref, taps_ref[:, cols], HALO)
            x_ref[rows, cols] = ((x1_ref[rows, cols] + silu) * valid_ref[rows, :]).astype(BF)
        if count > 1:
            outs[1][rows, :] = (normed(x_ref[rows, :].astype(F32)) * gain_ref[...]).astype(BF)
    rows = pl.ds(HALO, span - 2 * HALO)
    for source, target in zip(ins, outs):
        target[rows, :] = source[rows, :]


def edges(g, low, high, x1, taps, valid, gain, inners):
    span, width = x1.shape
    count = len(inners)
    return pl.pallas_call(
        functools.partial(edges_kernel, count),
        out_shape=(jax.ShapeDtypeStruct((span, width), BF),) * count,
        scratch_shapes=[pltpu.VMEM((3 * HALO, 128), F32)],
        compiler_params=params(),
        name="edges",
    )(g, low, high, x1, taps, valid, gain, *inners)


def along(value, by):
    size = lax.axis_size(SEQ)
    pairs = [(i, i + by) for i in range(size) if 0 <= i + by < size]
    return lax.ppermute(value, SEQ, pairs)


def weight_blocks(w, frames):
    rows, cols = w.shape
    zs, xs, yls, cores = (lax.axis_size(a) for a in ("z", "x", "yl", "core"))
    deep = rows // yls
    width = cols // 3
    group = width // xs
    at = lax.axis_index("yl") * deep
    col = lax.axis_index("x") * group
    own = jnp.concatenate(
        [lax.dynamic_slice(w, (at, part * width + col), (deep, group)) for part in (1, 2, 0)],
        axis=1,
    )
    half = zs // cores
    came = {}
    for k in range(1, half + 1):
        pairs = [(cores * z, cores * ((z + k) % zs)) for z in range(zs) if k < half]
        pairs += [(cores * z + 1, cores * ((z - k) % zs) + 1) for z in range(zs)]
        came[k] = lax.ppermute(own, ("z", "core"), pairs)
    first = lax.axis_index("core") == 0
    stack = jnp.concatenate(
        [
            jnp.where(first, came[k] if k else own, came[half - k])
            for k in range(half)
        ],
        axis=0,
    )
    stack, frames = lax.optimization_barrier((stack, frames))
    full = lax.all_gather(stack, ("yh",) + SEQ, axis=0, tiled=True)
    parts = lax.axis_size("yh") * yls
    return full.reshape(parts, xs, zs, deep, 3 * group), frames


def on_device(frames, arrival, lengths, attn_gain, w_qkv, w_out, conv_gain, conv_kernel):
    span = frames.shape[1]
    width = w_out.shape[0]
    group = lax.axis_index(DP)
    place = lax.axis_index(SEQ)
    groups = lax.axis_size(DP)
    w, frames = weight_blocks(w_qkv, frames)
    row_here = lax.dynamic_index_in_dim(arrival, place, 0, keepdims=False)
    chunks = frames.reshape(groups, span // groups, width)
    chunks = lax.all_to_all(chunks, DP, split_axis=0, concat_axis=0, tiled=True)
    chunks = pick(chunks, row_here)
    chunks = lax.all_to_all(chunks, DP, split_axis=0, concat_axis=0, tiled=True)
    x = chunks.reshape(span, width)

    length = lax.dynamic_index_in_dim(lengths, group, 0, keepdims=False)
    position = place * span + jnp.arange(span)
    own_valid = position < length
    left_valid = jnp.logical_and(position - span < length, place > 0)
    key_valid = jnp.concatenate([left_valid, own_valid])
    bias = jnp.where(key_valid, 0.0, -1e30).astype(BF)
    bias = jnp.where(jnp.arange(128)[None, :] == 0, bias[:, None], jnp.zeros((), BF))
    valid = own_valid.astype(F32)[:, None]
    gain_a = attn_gain[None, :]
    gain_c = conv_gain[None, :]
    taps = jnp.pad(conv_kernel, ((0, 1), (0, 0)))

    h = head(x, gain_a)
    for step in range(ITERS):
        last = step == ITERS - 1
        left = along(h, 1)
        if step == 0:
            z = lax.axis_index("z").astype(jnp.int32)[None]
            x1, g, w = opening(z, left, h, w, w_out, x, bias, gain_c, valid)
        else:
            x1, g = attend(left, project(h, w), w, w_out, x, bias, gain_c, valid)
        low = along(g[span - HALO :], 1)
        high = along(g[:HALO], -1)
        inners = inner(g, x1, taps, valid, gain_a, last)
        out = edges(g, low, high, x1, taps, valid, gain_a, inners)
        x = out[0]
        if not last:
            h = out[1]
    return x[None]


def solution(mesh):
    fine = Mesh(mesh.devices.reshape(8, 2, 2, 4, 2), DP + SEQ)
    placed = (P(DP, SEQ, None), P(), P(), P(), P(DP, None), P(), P(), P())
    return jax.shard_map(
        on_device, mesh=fine, in_specs=placed, out_specs=P(DP, SEQ, None), check_vma=False
    )
```

```python
import functools

import jax
import jax.numpy as jnp
from jax import lax
from jax.experimental import pallas as pl
from jax.experimental.pallas import tpu as pltpu
from jax.sharding import Mesh, PartitionSpec as P

HEAD = 64
KERNEL = 31
ITERS = 2
HALO = 16
EPS = 1e-05
DP = ("z", "yh")
SEQ = ("yl", "x", "core")
BF = jnp.bfloat16
F32 = jnp.float32
VMEM = 24 * 1024 * 1024


def params(**kw):
    return pltpu.CompilerParams(vmem_limit_bytes=VMEM, **kw)


def in_vmem(v):
    return pltpu.with_memory_space_constraint(v, pltpu.VMEM)


def in_hbm(v):
    return pltpu.with_memory_space_constraint(v, pltpu.HBM)


def normed(v):
    mean = jnp.mean(v, axis=-1, keepdims=True)
    d = v - mean
    var = jnp.mean(d * d, axis=-1, keepdims=True)
    return d * lax.rsqrt(var + EPS)


def pick_kernel(row_ref, in_ref, out_ref):
    for r in range(in_ref.shape[0]):
        out_ref[r] = in_ref[row_ref[r]]


def pick(chunks, row):
    return pl.pallas_call(
        pick_kernel,
        out_shape=jax.ShapeDtypeStruct(chunks.shape, chunks.dtype),
        in_specs=[
            pl.BlockSpec(memory_space=pltpu.SMEM),
            pl.BlockSpec(memory_space=pltpu.VMEM),
        ],
        out_specs=pl.BlockSpec(memory_space=pltpu.VMEM),
        compiler_params=params(),
        name="pick",
    )(row, chunks)


def head_kernel(x_ref, gain_ref, out_ref):
    out_ref[...] = (normed(x_ref[...].astype(F32)) * gain_ref[...]).astype(BF)


def head(x, gain):
    return pl.pallas_call(
        head_kernel,
        out_shape=jax.ShapeDtypeStruct(x.shape, BF),
        compiler_params=params(),
        name="head",
    )(x, gain)


def project_kernel(h_ref, w_ref, out_ref):
    for b in range(w_ref.shape[0]):
        out_ref[b] = jnp.dot(h_ref[...], w_ref[b], preferred_element_type=F32).astype(BF)


def project(h, w):
    blocks, _, cols = w.shape
    return pl.pallas_call(
        project_kernel,
        out_shape=pltpu.VMEM((blocks, h.shape[0], cols), BF),
        compiler_params=params(),
        name="project",
    )(h, in_vmem(w))


def heads(query, keys, values, bias):
    span = query.shape[0]
    lane = lax.broadcasted_iota(jnp.int32, (span, 128), 1)
    low = lane < HEAD
    tag = jnp.where(lane == 0, 1.0, 0.0).astype(BF)
    ones = jnp.ones((2 * span, 128), BF)
    outs = []
    for at in range(0, query.shape[1], 128):
        k = jnp.concatenate([keys[:, at : at + 128], bias], axis=1)
        v = jnp.concatenate([values[:, at : at + 128], ones], axis=1)
        q = query[:, at : at + 128] * jnp.asarray(HEAD ** (-0.5), BF)
        halves = []
        for mask in (low, jnp.logical_not(low)):
            qh = jnp.concatenate([jnp.where(mask, q, jnp.zeros_like(q)), tag], axis=1)
            s = lax.dot_general(qh, k, (((1,), (1,)), ((), ())), preferred_element_type=F32)
            top = jnp.max(s, axis=-1, keepdims=True)
            e = jnp.exp(s - top).astype(BF)
            o = jnp.dot(e, v, preferred_element_type=F32)
            halves.append(o[:, :128] / o[:, 128:])
        outs.append(jnp.where(low, halves[0], halves[1]).astype(BF))
    return jnp.concatenate(outs, axis=1)


def settle(ctx, wout_ref, x_ref, gain_ref, valid_ref, x1_ref, g_ref, acc_ref):
    b = pl.program_id(0)
    part = jnp.dot(ctx, wout_ref[...], preferred_element_type=F32)

    @pl.when(b == 0)
    def _():
        acc_ref[...] = x_ref[...].astype(F32) + part

    @pl.when(b > 0)
    def _():
        acc_ref[...] += part

    @pl.when(b == pl.num_programs(0) - 1)
    def _():
        x1 = acc_ref[...]
        x1_ref[...] = x1
        g_ref[...] = (normed(x1) * gain_ref[...] * valid_ref[...]).astype(BF)


def opening_kernel(
    z_ref, left_ref, h_ref, w_ref, wout_ref, x_ref, bias_ref, gain_ref, valid_ref,
    x1_ref, g_ref, wall_ref, acc_ref, both_ref, sem,
):
    b = pl.program_id(0)
    last = pl.num_programs(0) - 1
    span = h_ref.shape[0]
    group = wout_ref.shape[0]
    parts, _, zs, rows, _ = w_ref.shape

    def fetch(block):
        for part in range(parts):
            for z in range(zs):
                at = (z * parts + part) * rows
                pltpu.make_async_copy(
                    w_ref.at[part, block, lax.rem(z_ref[0] - z + zs, zs)],
                    wall_ref.at[block, pl.ds(at, rows)],
                    sem.at[block],
                ).start()

    @pl.when(b == 0)
    def _():
        fetch(0)
        both_ref[pl.ds(0, span), :] = left_ref[...]
        both_ref[pl.ds(span, span), :] = h_ref[...]

    @pl.when(b < last)
    def _():
        fetch(b + 1)

    pltpu.make_async_copy(wall_ref.at[b], wall_ref.at[b], sem.at[b]).wait()
    kv = jnp.dot(both_ref[...], wall_ref[b, :, : 2 * group], preferred_element_type=F32).astype(BF)
    q = jnp.dot(h_ref[...], wall_ref[b, :, 2 * group :], preferred_element_type=F32).astype(BF)
    ctx = heads(q, kv[:, :group], kv[:, group:], bias_ref[...])
    settle(ctx, wout_ref, x_ref, gain_ref, valid_ref, x1_ref, g_ref, acc_ref)


def whole(*shape):
    return pl.BlockSpec(shape, lambda b: (0,) * len(shape))


def opening(z, left, h, w, w_out, x, bias, gain, valid):
    parts, blocks, zs, rows, cols = w.shape
    span, width = x.shape
    group = width // blocks
    depth = parts * zs * rows
    return pl.pallas_call(
        opening_kernel,
        grid=(blocks,),
        out_shape=(
            jax.ShapeDtypeStruct((span, width), F32),
            jax.ShapeDtypeStruct((span, width), BF),
            pltpu.VMEM((blocks, depth, cols), BF),
        ),
        in_specs=[
            pl.BlockSpec(memory_space=pltpu.SMEM),
            whole(span, width),
            whole(span, width),
            pl.BlockSpec(memory_space=pl.ANY),
            pl.BlockSpec((group, width), lambda b: (b, 0)),
            whole(span, width),
            whole(2 * span, 128),
            whole(1, width),
            whole(span, 1),
        ],
        out_specs=(whole(span, width), whole(span, width), pl.BlockSpec(memory_space=pltpu.VMEM)),
        scratch_shapes=[
            pltpu.VMEM((span, width), F32),
            pltpu.VMEM((2 * span, width), BF),
            pltpu.SemaphoreType.DMA((blocks,)),
        ],
        compiler_params=params(),
        name="opening",
    )(z, left, h, w, in_hbm(w_out), x, bias, gain, valid)


def attend_kernel(
    left_ref, own_ref, w_ref, wout_ref, x_ref, bias_ref, gain_ref, valid_ref,
    x1_ref, g_ref, acc_ref,
):
    b = pl.program_id(0)
    group = wout_ref.shape[0]
    left = jnp.dot(left_ref[...], w_ref[b, :, : 2 * group], preferred_element_type=F32).astype(BF)
    own = own_ref[b]
    keys = jnp.concatenate([left[:, :group], own[:, :group]], axis=0)
    values = jnp.concatenate([left[:, group:], own[:, group : 2 * group]], axis=0)
    ctx = heads(own[:, 2 * group :], keys, values, bias_ref[...])
    settle(ctx, wout_ref, x_ref, gain_ref, valid_ref, x1_ref, g_ref, acc_ref)


def attend(left, own, w, w_out, x, bias, gain, valid):
    blocks = w.shape[0]
    span, width = x.shape
    group = width // blocks
    return pl.pallas_call(
        attend_kernel,
        grid=(blocks,),
        out_shape=(
            jax.ShapeDtypeStruct((span, width), F32),
            jax.ShapeDtypeStruct((span, width), BF),
        ),
        in_specs=[
            whole(span, width),
            pl.BlockSpec(memory_space=pltpu.VMEM),
            pl.BlockSpec(memory_space=pltpu.VMEM),
            pl.BlockSpec((group, width), lambda b: (b, 0)),
            whole(span, width),
            whole(2 * span, 128),
            whole(1, width),
            whole(span, 1),
        ],
        out_specs=(whole(span, width), whole(span, width)),
        scratch_shapes=[pltpu.VMEM((span, width), F32)],
        compiler_params=params(),
        name="attend",
    )(left, in_vmem(own), in_vmem(w), in_hbm(w_out), x, bias, gain, valid)


def taps_over(pad_ref, taps, rows):
    y = jnp.zeros((rows, 128), F32)
    for r in range(8):
        hits = [(j, (j + 1) // 8) for j in range(KERNEL) if (j + 1) % 8 == r]
        deep = max(m for _, m in hits)
        moved = pad_ref[pl.ds(r, rows + 8 * deep), :]
        for j, m in hits:
            y = y + taps[j : j + 1, :] * moved[8 * m : 8 * m + rows]
    return y / (1.0 + jnp.exp(-y))


def inner_kernel(g_ref, x1_ref, taps_ref, valid_ref, gain_ref, x_ref, *rest):
    pad_ref = rest[-1]
    span, width = x1_ref.shape
    rows = pl.ds(HALO, span - 2 * HALO)
    for c in range(width // 128):
        cols = pl.ds(128 * c, 128)
        pad_ref[...] = g_ref[:, cols].astype(F32)
        silu = taps_over(pad_ref, taps_ref[:, cols], span - 2 * HALO)
        x_ref[rows, cols] = ((x1_ref[rows, cols] + silu) * valid_ref[rows, :]).astype(BF)
    if len(rest) > 1:
        rest[0][rows, :] = (normed(x_ref[rows, :].astype(F32)) * gain_ref[...]).astype(BF)


def inner(g, x1, taps, valid, gain, last):
    span, width = x1.shape
    return pl.pallas_call(
        inner_kernel,
        out_shape=(jax.ShapeDtypeStruct((span, width), BF),) * (1 if last else 2),
        scratch_shapes=[pltpu.VMEM((span, 128), F32)],
        compiler_params=params(),
        name="inner",
    )(g, x1, taps, valid, gain)


def edges_kernel(count, g_ref, low_ref, high_ref, x1_ref, taps_ref, valid_ref, gain_ref, *rest):
    ins, outs, pad_ref = rest[:count], rest[count:-1], rest[-1]
    span, width = x1_ref.shape
    x_ref = outs[0]
    for at in (0, span - HALO):
        rows = pl.ds(at, HALO)
        for c in range(width // 128):
            cols = pl.ds(128 * c, 128)
            if at == 0:
                pad_ref[pl.ds(0, HALO), :] = low_ref[:, cols].astype(F32)
                pad_ref[pl.ds(HALO, 2 * HALO), :] = g_ref[pl.ds(0, 2 * HALO), cols].astype(F32)
            else:
                pad_ref[pl.ds(0, 2 * HALO), :] = g_ref[pl.ds(span - 2 * HALO, 2 * HALO), cols].astype(F32)
                pad_ref[pl.ds(2 * HALO, HALO), :] = high_ref[:, cols].astype(F32)
            silu = taps_over(pad_ref, taps_ref[:, cols], HALO)
            x_ref[rows, cols] = ((x1_ref[rows, cols] + silu) * valid_ref[rows, :]).astype(BF)
        if count > 1:
            outs[1][rows, :] = (normed(x_ref[rows, :].astype(F32)) * gain_ref[...]).astype(BF)
    rows = pl.ds(HALO, span - 2 * HALO)
    for source, target in zip(ins, outs):
        target[rows, :] = source[rows, :]


def edges(g, low, high, x1, taps, valid, gain, inners):
    span, width = x1.shape
    count = len(inners)
    return pl.pallas_call(
        functools.partial(edges_kernel, count),
        out_shape=(jax.ShapeDtypeStruct((span, width), BF),) * count,
        scratch_shapes=[pltpu.VMEM((3 * HALO, 128), F32)],
        compiler_params=params(),
        name="edges",
    )(g, low, high, x1, taps, valid, gain, *inners)


def along(value, by):
    size = lax.axis_size(SEQ)
    pairs = [(i, i + by) for i in range(size) if 0 <= i + by < size]
    return lax.ppermute(value, SEQ, pairs)


def weight_blocks(w, frames):
    rows, cols = w.shape
    zs, xs, yls, cores = (lax.axis_size(a) for a in ("z", "x", "yl", "core"))
    deep = rows // yls
    width = cols // 3
    group = width // xs
    at = lax.axis_index("yl") * deep
    col = lax.axis_index("x") * group
    own = jnp.concatenate(
        [lax.dynamic_slice(w, (at, part * width + col), (deep, group)) for part in (1, 2, 0)],
        axis=1,
    )
    half = zs // cores
    came = {}
    for k in range(1, half + 1):
        pairs = [(cores * z, cores * ((z + k) % zs)) for z in range(zs) if k < half]
        pairs += [(cores * z + 1, cores * ((z - k) % zs) + 1) for z in range(zs)]
        came[k] = lax.ppermute(own, ("z", "core"), pairs)
    first = lax.axis_index("core") == 0
    stack = jnp.concatenate(
        [
            jnp.where(first, came[k] if k else own, came[half - k])
            for k in range(half)
        ],
        axis=0,
    )
    stack, frames = lax.optimization_barrier((stack, frames))
    full = lax.all_gather(stack, ("yh",) + SEQ, axis=0, tiled=True)
    parts = lax.axis_size("yh") * yls
    return full.reshape(parts, xs, zs, deep, 3 * group), frames


def on_device(frames, arrival, lengths, attn_gain, w_qkv, w_out, conv_gain, conv_kernel):
    span = frames.shape[1]
    width = w_out.shape[0]
    group = lax.axis_index(DP)
    place = lax.axis_index(SEQ)
    groups = lax.axis_size(DP)
    w, frames = weight_blocks(w_qkv, frames)
    row_here = lax.dynamic_index_in_dim(arrival, place, 0, keepdims=False)
    chunks = frames.reshape(groups, span // groups, width)
    chunks = lax.all_to_all(chunks, DP, split_axis=0, concat_axis=0, tiled=True)
    chunks = pick(chunks, row_here)
    chunks = lax.all_to_all(chunks, DP, split_axis=0, concat_axis=0, tiled=True)
    x = chunks.reshape(span, width)

    length = lax.dynamic_index_in_dim(lengths, group, 0, keepdims=False)
    position = place * span + jnp.arange(span)
    own_valid = position < length
    left_valid = jnp.logical_and(position - span < length, place > 0)
    key_valid = jnp.concatenate([left_valid, own_valid])
    bias = jnp.where(key_valid, 0.0, -1e30).astype(BF)
    bias = jnp.where(jnp.arange(128)[None, :] == 0, bias[:, None], jnp.zeros((), BF))
    valid = own_valid.astype(F32)[:, None]
    gain_a = attn_gain[None, :]
    gain_c = conv_gain[None, :]
    taps = jnp.pad(conv_kernel, ((0, 1), (0, 0)))

    h = head(x, gain_a)
    for step in range(ITERS):
        last = step == ITERS - 1
        left = along(h, 1)
        if step == 0:
            z = lax.axis_index("z").astype(jnp.int32)[None]
            x1, g, w = opening(z, left, h, w, w_out, x, bias, gain_c, valid)
        else:
            x1, g = attend(left, project(h, w), w, w_out, x, bias, gain_c, valid)
        low = along(g[span - HALO :], 1)
        high = along(g[:HALO], -1)
        inners = inner(g, x1, taps, valid, gain_a, last)
        out = edges(g, low, high, x1, taps, valid, gain_a, inners)
        x = out[0]
        if not last:
            h = out[1]
    return x[None]


def solution(mesh):
    fine = Mesh(mesh.devices.reshape(8, 2, 2, 4, 2), DP + SEQ)
    placed = (P(DP, SEQ, None), P(), P(), P(), P(DP, None), P(), P(), P())
    return jax.shard_map(
        on_device, mesh=fine, in_specs=placed, out_specs=P(DP, SEQ, None), check_vma=False
    )
```

```python
import functools

import jax
import jax.numpy as jnp
from jax import lax
from jax.experimental import pallas as pl
from jax.experimental.pallas import tpu as pltpu
from jax.sharding import Mesh, PartitionSpec as P

HEAD = 64
KERNEL = 31
ITERS = 2
HALO = 16
EPS = 1e-05
DP = ("z", "yh")
SEQ = ("yl", "x", "core")
BF = jnp.bfloat16
F32 = jnp.float32
VMEM = 24 * 1024 * 1024


def params(**kw):
    return pltpu.CompilerParams(vmem_limit_bytes=VMEM, **kw)


def in_vmem(v):
    return pltpu.with_memory_space_constraint(v, pltpu.VMEM)


def in_hbm(v):
    return pltpu.with_memory_space_constraint(v, pltpu.HBM)


def normed(v):
    mean = jnp.mean(v, axis=-1, keepdims=True)
    d = v - mean
    var = jnp.mean(d * d, axis=-1, keepdims=True)
    return d * lax.rsqrt(var + EPS)


def pick_kernel(row_ref, in_ref, out_ref):
    for r in range(in_ref.shape[0]):
        out_ref[r] = in_ref[row_ref[r]]


def pick(chunks, row):
    return pl.pallas_call(
        pick_kernel,
        out_shape=jax.ShapeDtypeStruct(chunks.shape, chunks.dtype),
        in_specs=[
            pl.BlockSpec(memory_space=pltpu.SMEM),
            pl.BlockSpec(memory_space=pltpu.VMEM),
        ],
        out_specs=pl.BlockSpec(memory_space=pltpu.VMEM),
        compiler_params=params(),
        name="pick",
    )(row, chunks)


def head_kernel(x_ref, gain_ref, out_ref):
    out_ref[...] = (normed(x_ref[...].astype(F32)) * gain_ref[...]).astype(BF)


def head(x, gain):
    return pl.pallas_call(
        head_kernel,
        out_shape=jax.ShapeDtypeStruct(x.shape, BF),
        compiler_params=params(),
        name="head",
    )(x, gain)


def rows_of(h, w, wq, b):
    extra = wq.shape[1] // w.shape[0]
    main = jnp.dot(h, w[b], preferred_element_type=F32).astype(BF)
    rest = jnp.dot(h, wq[:, pl.ds(b * extra, extra)], preferred_element_type=F32).astype(BF)
    return main, rest


def project_kernel(h_ref, w_ref, wq_ref, out_ref):
    cols = w_ref.shape[2]
    for b in range(w_ref.shape[0]):
        main, rest = rows_of(h_ref[...], w_ref, wq_ref, b)
        out_ref[b, :, :cols] = main
        out_ref[b, :, cols:] = rest


def project(h, w, wq):
    blocks, _, cols = w.shape
    return pl.pallas_call(
        project_kernel,
        out_shape=pltpu.VMEM((blocks, h.shape[0], cols + wq.shape[1] // blocks), BF),
        compiler_params=params(),
        name="project",
    )(h, in_vmem(w), in_vmem(wq))


def opening_kernel(at_ref, h_ref, w_ref, mine_ref, other_ref, wall_ref, wq_ref, out_ref, sem):
    parts, blocks, zs, rows, cols = w_ref.shape
    half = mine_ref.shape[1]
    extra = wq_ref.shape[1] // blocks
    z, y, core = at_ref[0], at_ref[1], at_ref[2]

    def fetch(block):
        for part in range(parts):
            for to in range(zs):
                pltpu.make_async_copy(
                    w_ref.at[part, block, lax.rem(z - to + zs, zs)],
                    wall_ref.at[block, pl.ds((to * parts + part) * rows, rows)],
                    sem.at[block],
                ).start()

    def fetch_rest():
        for source, lane in ((mine_ref, core), (other_ref, 1 - core)):
            for step in range(parts):
                for slot in range(half):
                    to = lax.rem(z - (lane * half + slot) + zs, zs)
                    part = lax.rem(y + step, parts)
                    row = pl.multiple_of((to * parts + part) * rows, rows)
                    pltpu.make_async_copy(
                        source.at[step, slot], wq_ref.at[pl.ds(row, rows)], sem.at[blocks]
                    ).start()

    fetch(0)
    fetch_rest()
    fetch(1)
    for b in range(blocks):
        if b + 2 < blocks:
            fetch(b + 2)
        pltpu.make_async_copy(wall_ref.at[b], wall_ref.at[b], sem.at[b]).wait()
        out_ref[b, :, :cols] = jnp.dot(
            h_ref[...], wall_ref[b], preferred_element_type=F32
        ).astype(BF)
        if b == 0:
            pltpu.make_async_copy(wq_ref, wq_ref, sem.at[blocks]).wait()
        out_ref[b, :, cols:] = jnp.dot(
            h_ref[...], wq_ref[:, pl.ds(b * extra, extra)], preferred_element_type=F32
        ).astype(BF)


def opening(at, h, w, mine, other):
    parts, blocks, zs, rows, cols = w.shape
    depth = parts * zs * rows
    rest = mine.shape[-1]
    anywhere = pl.BlockSpec(memory_space=pl.ANY)
    return pl.pallas_call(
        opening_kernel,
        out_shape=(
            pltpu.VMEM((blocks, depth, cols), BF),
            pltpu.VMEM((depth, rest), BF),
            pltpu.VMEM((blocks, h.shape[0], cols + rest // blocks), BF),
        ),
        in_specs=[
            pl.BlockSpec(memory_space=pltpu.SMEM),
            pl.BlockSpec(memory_space=pltpu.VMEM),
            anywhere,
            anywhere,
            anywhere,
        ],
        out_specs=(pl.BlockSpec(memory_space=pltpu.VMEM),) * 3,
        scratch_shapes=[pltpu.SemaphoreType.DMA((blocks + 1,))],
        compiler_params=params(),
        name="opening",
    )(at, h, w, mine, other)


def heads(query, keys, values, bias):
    span = query.shape[0]
    lane = lax.broadcasted_iota(jnp.int32, (span, 128), 1)
    low = lane < HEAD
    tag = jnp.where(lane == 0, 1.0, 0.0).astype(BF)
    ones = jnp.ones((2 * span, 128), BF)
    outs = []
    for at in range(0, query.shape[1], 128):
        k = jnp.concatenate([keys[:, at : at + 128], bias], axis=1)
        v = jnp.concatenate([values[:, at : at + 128], ones], axis=1)
        q = query[:, at : at + 128] * jnp.asarray(HEAD ** (-0.5), BF)
        halves = []
        for mask in (low, jnp.logical_not(low)):
            qh = jnp.concatenate([jnp.where(mask, q, jnp.zeros_like(q)), tag], axis=1)
            s = lax.dot_general(qh, k, (((1,), (1,)), ((), ())), preferred_element_type=F32)
            top = jnp.max(s, axis=-1, keepdims=True)
            e = jnp.exp(s - top).astype(BF)
            o = jnp.dot(e, v, preferred_element_type=F32)
            halves.append(o[:, :128] / o[:, 128:])
        outs.append(jnp.where(low, halves[0], halves[1]).astype(BF))
    return jnp.concatenate(outs, axis=1)


def settle(ctx, wout_ref, x_ref, gain_ref, valid_ref, x1_ref, g_ref, acc_ref):
    b = pl.program_id(0)
    part = jnp.dot(ctx, wout_ref[...], preferred_element_type=F32)

    @pl.when(b == 0)
    def _():
        acc_ref[...] = x_ref[...].astype(F32) + part

    @pl.when(b > 0)
    def _():
        acc_ref[...] += part

    @pl.when(b == pl.num_programs(0) - 1)
    def _():
        x1 = acc_ref[...]
        x1_ref[...] = x1
        g_ref[...] = (normed(x1) * gain_ref[...] * valid_ref[...]).astype(BF)


def whole(*shape):
    return pl.BlockSpec(shape, lambda b: (0,) * len(shape))


def attend_kernel(
    left_ref, own_ref, w_ref, wout_ref, x_ref, bias_ref, gain_ref, valid_ref,
    x1_ref, g_ref, acc_ref,
):
    b = pl.program_id(0)
    group = wout_ref.shape[0]
    left = jnp.dot(left_ref[...], w_ref[b, :, : 2 * group], preferred_element_type=F32).astype(BF)
    own = own_ref[b]
    keys = jnp.concatenate([left[:, :group], own[:, :group]], axis=0)
    values = jnp.concatenate([left[:, group:], own[:, group : 2 * group]], axis=0)
    ctx = heads(own[:, 2 * group :], keys, values, bias_ref[...])
    settle(ctx, wout_ref, x_ref, gain_ref, valid_ref, x1_ref, g_ref, acc_ref)


def attend(left, own, w, w_out, x, bias, gain, valid):
    blocks = w.shape[0]
    span, width = x.shape
    group = width // blocks
    return pl.pallas_call(
        attend_kernel,
        grid=(blocks,),
        out_shape=(
            jax.ShapeDtypeStruct((span, width), F32),
            jax.ShapeDtypeStruct((span, width), BF),
        ),
        in_specs=[
            whole(span, width),
            pl.BlockSpec(memory_space=pltpu.VMEM),
            pl.BlockSpec(memory_space=pltpu.VMEM),
            pl.BlockSpec((group, width), lambda b: (b, 0)),
            whole(span, width),
            whole(2 * span, 128),
            whole(1, width),
            whole(span, 1),
        ],
        out_specs=(whole(span, width), whole(span, width)),
        scratch_shapes=[pltpu.VMEM((span, width), F32)],
        compiler_params=params(),
        name="attend",
    )(left, in_vmem(own), in_vmem(w), in_hbm(w_out), x, bias, gain, valid)


def taps_over(pad_ref, taps, rows):
    y = jnp.zeros((rows, 128), F32)
    for r in range(8):
        hits = [(j, (j + 1) // 8) for j in range(KERNEL) if (j + 1) % 8 == r]
        deep = max(m for _, m in hits)
        moved = pad_ref[pl.ds(r, rows + 8 * deep), :]
        for j, m in hits:
            y = y + taps[j : j + 1, :] * moved[8 * m : 8 * m + rows]
    return y / (1.0 + jnp.exp(-y))


def inner_kernel(g_ref, x1_ref, taps_ref, valid_ref, gain_ref, x_ref, *rest):
    pad_ref = rest[-1]
    span, width = x1_ref.shape
    rows = pl.ds(HALO, span - 2 * HALO)
    for c in range(width // 128):
        cols = pl.ds(128 * c, 128)
        pad_ref[...] = g_ref[:, cols].astype(F32)
        silu = taps_over(pad_ref, taps_ref[:, cols], span - 2 * HALO)
        x_ref[rows, cols] = ((x1_ref[rows, cols] + silu) * valid_ref[rows, :]).astype(BF)
    if len(rest) > 1:
        rest[0][rows, :] = (normed(x_ref[rows, :].astype(F32)) * gain_ref[...]).astype(BF)


def inner(g, x1, taps, valid, gain, last):
    span, width = x1.shape
    return pl.pallas_call(
        inner_kernel,
        out_shape=(jax.ShapeDtypeStruct((span, width), BF),) * (1 if last else 2),
        scratch_shapes=[pltpu.VMEM((span, 128), F32)],
        compiler_params=params(),
        name="inner",
    )(g, x1, taps, valid, gain)


def edges_kernel(count, g_ref, low_ref, high_ref, x1_ref, taps_ref, valid_ref, gain_ref, *rest):
    ins, outs, pad_ref = rest[:count], rest[count:-1], rest[-1]
    span, width = x1_ref.shape
    x_ref = outs[0]
    for at in (0, span - HALO):
        rows = pl.ds(at, HALO)
        for c in range(width // 128):
            cols = pl.ds(128 * c, 128)
            if at == 0:
                pad_ref[pl.ds(0, HALO), :] = low_ref[:, cols].astype(F32)
                pad_ref[pl.ds(HALO, 2 * HALO), :] = g_ref[pl.ds(0, 2 * HALO), cols].astype(F32)
            else:
                pad_ref[pl.ds(0, 2 * HALO), :] = g_ref[pl.ds(span - 2 * HALO, 2 * HALO), cols].astype(F32)
                pad_ref[pl.ds(2 * HALO, HALO), :] = high_ref[:, cols].astype(F32)
            silu = taps_over(pad_ref, taps_ref[:, cols], HALO)
            x_ref[rows, cols] = ((x1_ref[rows, cols] + silu) * valid_ref[rows, :]).astype(BF)
        if count > 1:
            outs[1][rows, :] = (normed(x_ref[rows, :].astype(F32)) * gain_ref[...]).astype(BF)
    rows = pl.ds(HALO, span - 2 * HALO)
    for source, target in zip(ins, outs):
        target[rows, :] = source[rows, :]


def edges(g, low, high, x1, taps, valid, gain, inners):
    span, width = x1.shape
    count = len(inners)
    return pl.pallas_call(
        functools.partial(edges_kernel, count),
        out_shape=(jax.ShapeDtypeStruct((span, width), BF),) * count,
        scratch_shapes=[pltpu.VMEM((3 * HALO, 128), F32)],
        compiler_params=params(),
        name="edges",
    )(g, low, high, x1, taps, valid, gain, *inners)


def along(value, by):
    size = lax.axis_size(SEQ)
    pairs = [(i, i + by) for i in range(size) if 0 <= i + by < size]
    return lax.ppermute(value, SEQ, pairs)


def carve_kernel(group, at_ref, w_ref, out_ref):
    width = w_ref.shape[1] // 3
    start = pl.multiple_of(at_ref[1] * group, 128)
    out_ref[:, :group] = w_ref[:, pl.ds(width + start, group)]
    out_ref[:, group : 2 * group] = w_ref[:, pl.ds(2 * width + start, group)]
    out_ref[:, 2 * group : 2 * group + 128] = w_ref[:, pl.ds(start, 128)]
    to = 2 * group + 128
    for x in range(width // group):
        out_ref[:, to : to + group - 128] = w_ref[:, x * group + 128 : (x + 1) * group]
        to += group - 128


def carve(at, w, deep, group):
    width = w.shape[1] // 3
    size = 2 * group + 128 + (width // group) * (group - 128)
    return pl.pallas_call(
        functools.partial(carve_kernel, group),
        grid_spec=pltpu.PrefetchScalarGridSpec(
            num_scalar_prefetch=1,
            grid=(1,),
            in_specs=[pl.BlockSpec((deep, w.shape[1]), lambda i, at: (at[0], 0))],
            out_specs=pl.BlockSpec((deep, size), lambda i, at: (0, 0)),
        ),
        out_shape=jax.ShapeDtypeStruct((deep, size), w.dtype),
        compiler_params=params(),
        name="carve",
    )(at, in_hbm(w))


def line_up_kernel(core_ref, *refs):
    came, (near_ref, far_ref) = refs[:-2], refs[-2:]
    half = len(came) - 1
    deep = came[0].shape[0]
    cut = near_ref.shape[1]
    for lane in range(2):

        @pl.when(core_ref[0] == lane)
        def _():
            for k in range(half):
                piece = came[half - k] if lane else came[k]
                near_ref[pl.ds(k * deep, deep), :] = piece[:, :cut]
                far_ref[pl.ds(k * deep, deep), :] = piece[:, cut:]


def line_up(core, came, cut):
    deep, size = came[0].shape
    rows = deep * (len(came) - 1)
    space = pl.BlockSpec(memory_space=pltpu.VMEM)
    return pl.pallas_call(
        line_up_kernel,
        out_shape=(
            jax.ShapeDtypeStruct((rows, cut), BF),
            jax.ShapeDtypeStruct((rows, size - cut), BF),
        ),
        in_specs=[pl.BlockSpec(memory_space=pltpu.SMEM)] + [space] * len(came),
        out_specs=(space, space),
        compiler_params=params(),
        name="line_up",
    )(core, *came)


def weight_blocks(w, frames):
    rows, cols = w.shape
    zs, xs, yhs, yls, cores = (lax.axis_size(a) for a in ("z", "x", "yh", "yl", "core"))
    deep = rows // yls
    group = cols // 3 // xs
    cut = 2 * group + 128
    at = jnp.stack([lax.axis_index("yl"), lax.axis_index("x")]).astype(jnp.int32)
    own = carve(at, w, deep, group)
    half = zs // cores
    came = []
    for k in range(1, half + 1):
        pairs = [(cores * z, cores * ((z + k) % zs)) for z in range(zs) if k < half]
        pairs += [(cores * z + 1, cores * ((z - k) % zs) + 1) for z in range(zs)]
        came.append(lax.ppermute(own, ("z", "core"), pairs))
    near, far = line_up(lax.axis_index("core").astype(jnp.int32)[None], [own] + came, cut)
    near, far, frames = lax.optimization_barrier((near, far, frames))
    parts = yhs * yls
    turned = [far] + [
        lax.ppermute(far, ("yh", "yl"), [(i, (i - k) % parts) for i in range(parts)])
        for k in range(1, parts)
    ]
    full = lax.all_gather(near, ("yh",) + SEQ, axis=0, tiled=True)
    turned = jnp.stack(turned).reshape(parts, half, deep, -1)
    return full.reshape(parts, xs, zs, deep, cut), turned, frames


def on_device(frames, arrival, lengths, attn_gain, w_qkv, w_out, conv_gain, conv_kernel):
    span = frames.shape[1]
    width = w_out.shape[0]
    group = lax.axis_index(DP)
    place = lax.axis_index(SEQ)
    groups = lax.axis_size(DP)
    w, mine, frames = weight_blocks(w_qkv, frames)
    row_here = lax.dynamic_index_in_dim(arrival, place, 0, keepdims=False)
    chunks = frames.reshape(groups, span // groups, width)
    chunks = lax.all_to_all(chunks, DP, split_axis=0, concat_axis=0, tiled=True)
    chunks = pick(chunks, row_here)
    chunks, mine = lax.optimization_barrier((chunks, mine))
    other = lax.ppermute(mine, "core", [(0, 1), (1, 0)])
    chunks = lax.all_to_all(chunks, DP, split_axis=0, concat_axis=0, tiled=True)
    x = chunks.reshape(span, width)

    length = lax.dynamic_index_in_dim(lengths, group, 0, keepdims=False)
    position = place * span + jnp.arange(span)
    own_valid = position < length
    left_valid = jnp.logical_and(position - span < length, place > 0)
    key_valid = jnp.concatenate([left_valid, own_valid])
    bias = jnp.where(key_valid, 0.0, -1e30).astype(BF)
    bias = jnp.where(jnp.arange(128)[None, :] == 0, bias[:, None], jnp.zeros((), BF))
    valid = own_valid.astype(F32)[:, None]
    gain_a = attn_gain[None, :]
    gain_c = conv_gain[None, :]
    taps = jnp.pad(conv_kernel, ((0, 1), (0, 0)))

    h = head(x, gain_a)
    for step in range(ITERS):
        last = step == ITERS - 1
        left = along(h, 1)
        if step == 0:
            at = [lax.axis_index("z"), lax.axis_index(("yh", "yl")), lax.axis_index("core")]
            w, wq, own = opening(jnp.stack(at).astype(jnp.int32), h, w, mine, other)
        else:
            own = project(h, w, wq)
        x1, g = attend(left, own, w, w_out, x, bias, gain_c, valid)
        low = along(g[span - HALO :], 1)
        high = along(g[:HALO], -1)
        inners = inner(g, x1, taps, valid, gain_a, last)
        out = edges(g, low, high, x1, taps, valid, gain_a, inners)
        x = out[0]
        if not last:
            h = out[1]
    return x[None]


def solution(mesh):
    fine = Mesh(mesh.devices.reshape(8, 2, 2, 4, 2), DP + SEQ)
    placed = (P(DP, SEQ, None), P(), P(), P(), P(DP, None), P(), P(), P())
    return jax.shard_map(
        on_device, mesh=fine, in_specs=placed, out_specs=P(DP, SEQ, None), check_vma=False
    )
```

```python
import functools

import jax
import jax.numpy as jnp
from jax import lax
from jax.experimental import pallas as pl
from jax.experimental.pallas import tpu as pltpu
from jax.sharding import Mesh, PartitionSpec as P

HEAD = 64
KERNEL = 31
ITERS = 2
HALO = 16
EPS = 1e-05
DP = ("z", "yh")
SEQ = ("yl", "x", "core")
BF = jnp.bfloat16
F32 = jnp.float32
VMEM = 24 * 1024 * 1024


def params(**kw):
    return pltpu.CompilerParams(vmem_limit_bytes=VMEM, **kw)


def in_vmem(v):
    return pltpu.with_memory_space_constraint(v, pltpu.VMEM)


def in_hbm(v):
    return pltpu.with_memory_space_constraint(v, pltpu.HBM)


def normed(v):
    mean = jnp.mean(v, axis=-1, keepdims=True)
    d = v - mean
    var = jnp.mean(d * d, axis=-1, keepdims=True)
    return d * lax.rsqrt(var + EPS)


def pick_kernel(row_ref, in_ref, out_ref):
    for r in range(in_ref.shape[0]):
        out_ref[r] = in_ref[row_ref[r]]


def pick(chunks, row):
    return pl.pallas_call(
        pick_kernel,
        out_shape=jax.ShapeDtypeStruct(chunks.shape, chunks.dtype),
        in_specs=[
            pl.BlockSpec(memory_space=pltpu.SMEM),
            pl.BlockSpec(memory_space=pltpu.VMEM),
        ],
        out_specs=pl.BlockSpec(memory_space=pltpu.VMEM),
        compiler_params=params(),
        name="pick",
    )(row, chunks)


def head_kernel(x_ref, gain_ref, out_ref):
    out_ref[...] = (normed(x_ref[...].astype(F32)) * gain_ref[...]).astype(BF)


def head(x, gain):
    return pl.pallas_call(
        head_kernel,
        out_shape=jax.ShapeDtypeStruct(x.shape, BF),
        compiler_params=params(),
        name="head",
    )(x, gain)


def project_kernel(h_ref, w_ref, out_ref):
    for b in range(w_ref.shape[0]):
        out_ref[b] = jnp.dot(h_ref[...], w_ref[b], preferred_element_type=F32).astype(BF)


def project(h, w):
    blocks, _, cols = w.shape
    return pl.pallas_call(
        project_kernel,
        out_shape=pltpu.VMEM((blocks, h.shape[0], cols), BF),
        compiler_params=params(),
        name="project",
    )(h, in_vmem(w))


def heads(query, keys, values, bias):
    span = query.shape[0]
    lane = lax.broadcasted_iota(jnp.int32, (span, 128), 1)
    low = lane < HEAD
    tag = jnp.where(lane == 0, 1.0, 0.0).astype(BF)
    ones = jnp.ones((2 * span, 128), BF)
    outs = []
    for at in range(0, query.shape[1], 128):
        k = jnp.concatenate([keys[:, at : at + 128], bias], axis=1)
        v = jnp.concatenate([values[:, at : at + 128], ones], axis=1)
        q = query[:, at : at + 128] * jnp.asarray(HEAD ** (-0.5), BF)
        halves = []
        for mask in (low, jnp.logical_not(low)):
            qh = jnp.concatenate([jnp.where(mask, q, jnp.zeros_like(q)), tag], axis=1)
            s = lax.dot_general(qh, k, (((1,), (1,)), ((), ())), preferred_element_type=F32)
            top = jnp.max(s, axis=-1, keepdims=True)
            e = jnp.exp(s - top).astype(BF)
            o = jnp.dot(e, v, preferred_element_type=F32)
            halves.append(o[:, :128] / o[:, 128:])
        outs.append(jnp.where(low, halves[0], halves[1]).astype(BF))
    return jnp.concatenate(outs, axis=1)


def settle(ctx, wout_ref, x_ref, gain_ref, valid_ref, x1_ref, g_ref, ctx_ref):
    b = pl.program_id(0)
    group = ctx.shape[1]
    ctx_ref[:, pl.ds(pl.multiple_of(b * group, group), group)] = ctx

    @pl.when(b == pl.num_programs(0) - 1)
    def _():
        x1 = x_ref[...].astype(F32) + jnp.dot(
            ctx_ref[...], wout_ref[...], preferred_element_type=F32
        )
        x1_ref[...] = x1
        g_ref[...] = (normed(x1) * gain_ref[...] * valid_ref[...]).astype(BF)


def opening_kernel(
    z_ref, left_ref, h_ref, w_ref, wout_ref, x_ref, bias_ref, gain_ref, valid_ref,
    x1_ref, g_ref, wall_ref, ctx_ref, both_ref, sem,
):
    b = pl.program_id(0)
    last = pl.num_programs(0) - 1
    span = h_ref.shape[0]
    group = wout_ref.shape[0] // w_ref.shape[0]
    _, parts, zs, rows, _ = w_ref.shape

    def fetch(block):
        for part in range(parts):
            for z in range(zs):
                at = (z * parts + part) * rows
                pltpu.make_async_copy(
                    w_ref.at[block, part, lax.rem(z_ref[0] - z + zs, zs)],
                    wall_ref.at[block, pl.ds(at, rows)],
                    sem.at[block],
                ).start()

    @pl.when(b == 0)
    def _():
        fetch(0)
        both_ref[pl.ds(0, span), :] = left_ref[...]
        both_ref[pl.ds(span, span), :] = h_ref[...]

    @pl.when(b < last)
    def _():
        fetch(b + 1)

    pltpu.make_async_copy(wall_ref.at[b], wall_ref.at[b], sem.at[b]).wait()
    kv = jnp.dot(both_ref[...], wall_ref[b, :, : 2 * group], preferred_element_type=F32).astype(BF)
    q = jnp.dot(h_ref[...], wall_ref[b, :, 2 * group :], preferred_element_type=F32).astype(BF)
    ctx = heads(q, kv[:, :group], kv[:, group:], bias_ref[...])
    settle(ctx, wout_ref, x_ref, gain_ref, valid_ref, x1_ref, g_ref, ctx_ref)


def whole(*shape):
    return pl.BlockSpec(shape, lambda b: (0,) * len(shape))


def opening(z, left, h, w, w_out, x, bias, gain, valid):
    blocks, parts, zs, rows, cols = w.shape
    span, width = x.shape
    group = width // blocks
    depth = parts * zs * rows
    return pl.pallas_call(
        opening_kernel,
        grid=(blocks,),
        out_shape=(
            jax.ShapeDtypeStruct((span, width), F32),
            jax.ShapeDtypeStruct((span, width), BF),
            pltpu.VMEM((blocks, depth, cols), BF),
        ),
        in_specs=[
            pl.BlockSpec(memory_space=pltpu.SMEM),
            whole(span, width),
            whole(span, width),
            pl.BlockSpec(memory_space=pl.ANY),
            whole(width, width),
            whole(span, width),
            whole(2 * span, 128),
            whole(1, width),
            whole(span, 1),
        ],
        out_specs=(whole(span, width), whole(span, width), pl.BlockSpec(memory_space=pltpu.VMEM)),
        scratch_shapes=[
            pltpu.VMEM((span, width), BF),
            pltpu.VMEM((2 * span, width), BF),
            pltpu.SemaphoreType.DMA((blocks,)),
        ],
        compiler_params=params(),
        name="opening",
    )(z, left, h, w, in_hbm(w_out), x, bias, gain, valid)


def attend_kernel(
    inner_ref, edge_ref, own_ref, w_ref, wout_ref, x_ref, bias_ref, gain_ref, valid_ref,
    x1_ref, g_ref, ctx_ref, left_ref,
):
    b = pl.program_id(0)
    group = wout_ref.shape[0] // w_ref.shape[0]
    span = left_ref.shape[0]

    @pl.when(b == 0)
    def _():
        left_ref[pl.ds(0, HALO), :] = edge_ref[pl.ds(0, HALO), :]
        left_ref[pl.ds(HALO, span - 2 * HALO), :] = inner_ref[...]
        left_ref[pl.ds(span - HALO, HALO), :] = edge_ref[pl.ds(HALO, HALO), :]

    left = jnp.dot(left_ref[...], w_ref[b, :, : 2 * group], preferred_element_type=F32).astype(BF)
    own = own_ref[b]
    keys = jnp.concatenate([left[:, :group], own[:, :group]], axis=0)
    values = jnp.concatenate([left[:, group:], own[:, group : 2 * group]], axis=0)
    ctx = heads(own[:, 2 * group :], keys, values, bias_ref[...])
    settle(ctx, wout_ref, x_ref, gain_ref, valid_ref, x1_ref, g_ref, ctx_ref)


def attend(left_inner, left_edge, own, w, w_out, x, bias, gain, valid):
    blocks = w.shape[0]
    span, width = x.shape
    group = width // blocks
    return pl.pallas_call(
        attend_kernel,
        grid=(blocks,),
        out_shape=(
            jax.ShapeDtypeStruct((span, width), F32),
            jax.ShapeDtypeStruct((span, width), BF),
        ),
        in_specs=[
            whole(span - 2 * HALO, width),
            whole(2 * HALO, width),
            pl.BlockSpec(memory_space=pltpu.VMEM),
            pl.BlockSpec(memory_space=pltpu.VMEM),
            whole(width, width),
            whole(span, width),
            whole(2 * span, 128),
            whole(1, width),
            whole(span, 1),
        ],
        out_specs=(whole(span, width), whole(span, width)),
        scratch_shapes=[pltpu.VMEM((span, width), BF), pltpu.VMEM((span, width), BF)],
        compiler_params=params(),
        name="attend",
    )(left_inner, left_edge, in_vmem(own), in_vmem(w), in_hbm(w_out), x, bias, gain, valid)


def taps_over(pad_ref, taps, rows):
    y = jnp.zeros((rows, 128), F32)
    for r in range(8):
        hits = [(j, (j + 1) // 8) for j in range(KERNEL) if (j + 1) % 8 == r]
        deep = max(m for _, m in hits)
        moved = pad_ref[pl.ds(r, rows + 8 * deep), :]
        for j, m in hits:
            y = y + taps[j : j + 1, :] * moved[8 * m : 8 * m + rows]
    return y / (1.0 + jnp.exp(-y))


def inner_kernel(g_ref, x1_ref, taps_ref, valid_ref, gain_ref, x_ref, *rest):
    pad_ref = rest[-1]
    span, width = x1_ref.shape
    rows = pl.ds(HALO, span - 2 * HALO)
    for c in range(width // 128):
        cols = pl.ds(128 * c, 128)
        pad_ref[...] = g_ref[:, cols].astype(F32)
        silu = taps_over(pad_ref, taps_ref[:, cols], span - 2 * HALO)
        x_ref[:, cols] = ((x1_ref[rows, cols] + silu) * valid_ref[rows, :]).astype(BF)
    if len(rest) > 1:
        rest[0][...] = (normed(x_ref[...].astype(F32)) * gain_ref[...]).astype(BF)


def inner(g, x1, taps, valid, gain, last):
    span, width = x1.shape
    out = jax.ShapeDtypeStruct((span - 2 * HALO, width), BF)
    return pl.pallas_call(
        inner_kernel,
        out_shape=(out,) * (1 if last else 2),
        scratch_shapes=[pltpu.VMEM((span, 128), F32)],
        compiler_params=params(),
        name="inner",
    )(g, x1, taps, valid, gain)


def edges_kernel(count, g_ref, low_ref, high_ref, x1_ref, taps_ref, valid_ref, gain_ref, *rest):
    ins, outs, pad_ref = rest[:count], rest[count:-1], rest[-1]
    if count > 1:
        outs, edge_ref = outs[:-1], outs[-1]
    span, width = x1_ref.shape
    x_ref = outs[0]
    for at in (0, span - HALO):
        rows = pl.ds(at, HALO)
        for c in range(width // 128):
            cols = pl.ds(128 * c, 128)
            if at == 0:
                pad_ref[pl.ds(0, HALO), :] = low_ref[:, cols].astype(F32)
                pad_ref[pl.ds(HALO, 2 * HALO), :] = g_ref[pl.ds(0, 2 * HALO), cols].astype(F32)
            else:
                pad_ref[pl.ds(0, 2 * HALO), :] = g_ref[pl.ds(span - 2 * HALO, 2 * HALO), cols].astype(F32)
                pad_ref[pl.ds(2 * HALO, HALO), :] = high_ref[:, cols].astype(F32)
            silu = taps_over(pad_ref, taps_ref[:, cols], HALO)
            x_ref[rows, cols] = ((x1_ref[rows, cols] + silu) * valid_ref[rows, :]).astype(BF)
        if count > 1:
            h = (normed(x_ref[rows, :].astype(F32)) * gain_ref[...]).astype(BF)
            outs[1][rows, :] = h
            edge_ref[pl.ds(HALO if at else 0, HALO), :] = h
    rows = pl.ds(HALO, span - 2 * HALO)
    for source, target in zip(ins, outs):
        target[rows, :] = source[...]


def edges(g, low, high, x1, taps, valid, gain, inners):
    span, width = x1.shape
    count = len(inners)
    return pl.pallas_call(
        functools.partial(edges_kernel, count),
        out_shape=(jax.ShapeDtypeStruct((span, width), BF),) * count
        + (jax.ShapeDtypeStruct((2 * HALO, width), BF),) * (count - 1),
        scratch_shapes=[pltpu.VMEM((3 * HALO, 128), F32)],
        compiler_params=params(),
        name="edges",
    )(g, low, high, x1, taps, valid, gain, *inners)


def along(value, by):
    size = lax.axis_size(SEQ)
    pairs = [(i, i + by) for i in range(size) if 0 <= i + by < size]
    return lax.ppermute(value, SEQ, pairs)


def weight_blocks(w, frames):
    rows, cols = w.shape
    zs, xs, yls, cores = (lax.axis_size(a) for a in ("z", "x", "yl", "core"))
    deep = rows // yls
    width = cols // 3
    group = width // xs
    at = lax.axis_index("yl") * deep
    col = lax.axis_index("x") * group
    own = jnp.concatenate(
        [lax.dynamic_slice(w, (at, part * width + col), (deep, group)) for part in (1, 2, 0)],
        axis=1,
    )
    half = zs // cores
    came = {}
    for k in range(1, half + 1):
        pairs = [(cores * z, cores * ((z + k) % zs)) for z in range(zs) if k < half]
        pairs += [(cores * z + 1, cores * ((z - k) % zs) + 1) for z in range(zs)]
        came[k] = lax.ppermute(own, ("z", "core"), pairs)
    first = lax.axis_index("core") == 0
    stack = jnp.concatenate(
        [
            jnp.where(first, came[k] if k else own, came[half - k])
            for k in range(half)
        ],
        axis=0,
    )
    stack, frames = lax.optimization_barrier((stack, frames))
    full = lax.all_gather(stack, ("x", "yh", "yl", "core"), axis=0, tiled=True)
    parts = lax.axis_size("yh") * yls
    return full.reshape(xs, parts, zs, deep, 3 * group), frames


def on_device(frames, arrival, lengths, attn_gain, w_qkv, w_out, conv_gain, conv_kernel):
    span = frames.shape[1]
    width = w_out.shape[0]
    group = lax.axis_index(DP)
    place = lax.axis_index(SEQ)
    groups = lax.axis_size(DP)
    w, frames = weight_blocks(w_qkv, frames)
    row_here = lax.dynamic_index_in_dim(arrival, place, 0, keepdims=False)
    chunks = frames.reshape(groups, span // groups, width)
    chunks = lax.all_to_all(chunks, DP, split_axis=0, concat_axis=0, tiled=True)
    chunks = pick(chunks, row_here)
    chunks = lax.all_to_all(chunks, DP, split_axis=0, concat_axis=0, tiled=True)
    x = chunks.reshape(span, width)

    length = lax.dynamic_index_in_dim(lengths, group, 0, keepdims=False)
    position = place * span + jnp.arange(span)
    own_valid = position < length
    left_valid = jnp.logical_and(position - span < length, place > 0)
    key_valid = jnp.concatenate([left_valid, own_valid])
    bias = jnp.where(key_valid, 0.0, -1e30).astype(BF)
    bias = jnp.where(jnp.arange(128)[None, :] == 0, bias[:, None], jnp.zeros((), BF))
    valid = own_valid.astype(F32)[:, None]
    gain_a = attn_gain[None, :]
    gain_c = conv_gain[None, :]
    taps = jnp.pad(conv_kernel, ((0, 1), (0, 0)))

    h = head(x, gain_a)
    for step in range(ITERS):
        last = step == ITERS - 1
        if step == 0:
            left = along(h, 1)
            z = lax.axis_index("z").astype(jnp.int32)[None]
            x1, g, w = opening(z, left, h, w, w_out, x, bias, gain_c, valid)
        else:
            left_edge = along(edge, 1)
            x1, g = attend(
                left_inner, left_edge, project(h, w), w, w_out, x, bias, gain_c, valid
            )
        low = along(g[span - HALO :], 1)
        high = along(g[:HALO], -1)
        inners = inner(g, x1, taps, valid, gain_a, last)
        if not last:
            h_inner, low, high = lax.optimization_barrier((inners[1], low, high))
            inners = (inners[0], h_inner)
            left_inner = along(h_inner, 1)
        out = edges(g, low, high, x1, taps, valid, gain_a, inners)
        x = out[0]
        if not last:
            h, edge = out[1:]
    return x[None]


def solution(mesh):
    fine = Mesh(mesh.devices.reshape(8, 2, 2, 4, 2), DP + SEQ)
    placed = (P(DP, SEQ, None), P(), P(), P(), P(DP, None), P(), P(), P())
    return jax.shard_map(
        on_device, mesh=fine, in_specs=placed, out_specs=P(DP, SEQ, None), check_vma=False
    )
```

```python
import functools

import jax
import jax.numpy as jnp
from jax import lax
from jax.experimental import pallas as pl
from jax.experimental.pallas import tpu as pltpu
from jax.sharding import Mesh, PartitionSpec as P

HEAD = 64
KERNEL = 31
ITERS = 2
HALO = 16
EPS = 1e-05
DP = ("z", "yh")
SEQ = ("yl", "x", "core")
BF = jnp.bfloat16
F32 = jnp.float32
VMEM = 24 * 1024 * 1024


def params(**kw):
    return pltpu.CompilerParams(vmem_limit_bytes=VMEM, **kw)


def in_vmem(v):
    return pltpu.with_memory_space_constraint(v, pltpu.VMEM)


def in_hbm(v):
    return pltpu.with_memory_space_constraint(v, pltpu.HBM)


def normed(v):
    mean = jnp.mean(v, axis=-1, keepdims=True)
    d = v - mean
    var = jnp.mean(d * d, axis=-1, keepdims=True)
    return d * lax.rsqrt(var + EPS)


def pick_kernel(row_ref, in_ref, out_ref):
    for r in range(in_ref.shape[0]):
        out_ref[r] = in_ref[row_ref[r]]


def pick(chunks, row):
    return pl.pallas_call(
        pick_kernel,
        out_shape=jax.ShapeDtypeStruct(chunks.shape, chunks.dtype),
        in_specs=[
            pl.BlockSpec(memory_space=pltpu.SMEM),
            pl.BlockSpec(memory_space=pltpu.VMEM),
        ],
        out_specs=pl.BlockSpec(memory_space=pltpu.VMEM),
        compiler_params=params(),
        name="pick",
    )(row, chunks)


def head_kernel(x_ref, gain_ref, out_ref, inner_ref, edge_ref):
    span = x_ref.shape[0]
    h = (normed(x_ref[...].astype(F32)) * gain_ref[...]).astype(BF)
    out_ref[...] = h
    inner_ref[...] = h[HALO : span - HALO]
    edge_ref[pl.ds(0, HALO), :] = h[:HALO]
    edge_ref[pl.ds(HALO, HALO), :] = h[span - HALO :]


def head(x, gain):
    span, width = x.shape
    return pl.pallas_call(
        head_kernel,
        out_shape=tuple(
            jax.ShapeDtypeStruct((rows, width), BF)
            for rows in (span, span - 2 * HALO, 2 * HALO)
        ),
        compiler_params=params(),
        name="head",
    )(x, gain)


def project_kernel(h_ref, w_ref, out_ref):
    for b in range(w_ref.shape[0]):
        out_ref[b] = jnp.dot(h_ref[...], w_ref[b], preferred_element_type=F32).astype(BF)


def project(h, w):
    blocks, _, cols = w.shape
    return pl.pallas_call(
        project_kernel,
        out_shape=pltpu.VMEM((blocks, h.shape[0], cols), BF),
        compiler_params=params(),
        name="project",
    )(h, in_vmem(w))


def heads(query, keys, values, bias):
    span = query.shape[0]
    lane = lax.broadcasted_iota(jnp.int32, (span, 128), 1)
    low = lane < HEAD
    tag = jnp.where(lane == 0, 1.0, 0.0).astype(BF)
    ones = jnp.ones((2 * span, 128), BF)
    outs = []
    for at in range(0, query.shape[1], 128):
        k = jnp.concatenate([keys[:, at : at + 128], bias], axis=1)
        v = jnp.concatenate([values[:, at : at + 128], ones], axis=1)
        q = query[:, at : at + 128] * jnp.asarray(HEAD ** (-0.5), BF)
        halves = []
        for mask in (low, jnp.logical_not(low)):
            qh = jnp.concatenate([jnp.where(mask, q, jnp.zeros_like(q)), tag], axis=1)
            s = lax.dot_general(qh, k, (((1,), (1,)), ((), ())), preferred_element_type=F32)
            top = jnp.max(s, axis=-1, keepdims=True)
            e = jnp.exp(s - top).astype(BF)
            o = jnp.dot(e, v, preferred_element_type=F32)
            halves.append(o[:, :128] / o[:, 128:])
        outs.append(jnp.where(low, halves[0], halves[1]).astype(BF))
    return jnp.concatenate(outs, axis=1)


def settle(ctx, wout_ref, x_ref, gain_ref, valid_ref, x1_ref, g_ref, ctx_ref):
    b = pl.program_id(0)
    group = ctx.shape[1]
    ctx_ref[:, pl.ds(pl.multiple_of(b * group, group), group)] = ctx

    @pl.when(b == pl.num_programs(0) - 1)
    def _():
        x1 = x_ref[...].astype(F32) + jnp.dot(
            ctx_ref[...], wout_ref[...], preferred_element_type=F32
        )
        x1_ref[...] = x1
        g_ref[...] = (normed(x1) * gain_ref[...] * valid_ref[...]).astype(BF)


OFFSETS = (0, 3, 1, 2)


def opening_kernel(at_ref, h_ref, *refs):
    mine, other = refs[:8], refs[8:16]
    wall_ref, out_ref, sem = refs[16:]
    blocks = wall_ref.shape[0]
    half, rows = mine[0].shape[1:3]
    z, y, x, core = (at_ref[i] for i in range(4))

    def unit(held, j, u):
        return held[2 * j + u // 2].at[u % 2]

    def fetch(b):
        block = lax.rem(x + OFFSETS[b], blocks)
        for lane in range(2):
            for held, here in ((mine, core == lane), (other, core != lane)):

                @pl.when(here)
                def _():
                    for k in range(len(OFFSETS)):
                        source = unit(held, b, k) if lane else unit(held, k, b)
                        part = lax.rem(y + OFFSETS[k], len(OFFSETS))
                        for slot in range(half):
                            to = lax.rem(z + 2 * half - (lane * half + slot), 2 * half)
                            row = pl.multiple_of((to * len(OFFSETS) + part) * rows, rows)
                            pltpu.make_async_copy(
                                source.at[slot], wall_ref.at[block, pl.ds(row, rows)], sem.at[b]
                            ).start()

    fetch(0)
    for b in range(blocks):
        if b + 1 < blocks:
            fetch(b + 1)
        block = lax.rem(x + OFFSETS[b], blocks)
        pltpu.make_async_copy(wall_ref.at[block], wall_ref.at[block], sem.at[b]).wait()
        out_ref[block] = jnp.dot(
            h_ref[...], wall_ref[block], preferred_element_type=F32
        ).astype(BF)


def opening(at, h, mine, other):
    _, half, rows, cols = mine[0].shape
    depth = 2 * half * len(OFFSETS) * rows
    blocks = len(OFFSETS)
    space = pl.BlockSpec(memory_space=pltpu.VMEM)
    anywhere = pl.BlockSpec(memory_space=pl.ANY)
    return pl.pallas_call(
        opening_kernel,
        out_shape=(
            pltpu.VMEM((blocks, depth, cols), BF),
            pltpu.VMEM((blocks, h.shape[0], cols), BF),
        ),
        in_specs=[pl.BlockSpec(memory_space=pltpu.SMEM), space] + [anywhere] * 16,
        out_specs=(space, space),
        scratch_shapes=[pltpu.SemaphoreType.DMA((blocks,))],
        compiler_params=params(),
        name="opening",
    )(at, h, *(in_hbm(v) for v in (*mine, *other)))


def whole(*shape):
    return pl.BlockSpec(shape, lambda b: (0,) * len(shape))


def attend_kernel(
    inner_ref, edge_ref, own_ref, w_ref, wout_ref, x_ref, bias_ref, gain_ref, valid_ref,
    x1_ref, g_ref, ctx_ref, left_ref,
):
    b = pl.program_id(0)
    group = wout_ref.shape[0] // w_ref.shape[0]
    span = left_ref.shape[0]

    @pl.when(b == 0)
    def _():
        left_ref[pl.ds(0, HALO), :] = edge_ref[pl.ds(0, HALO), :]
        left_ref[pl.ds(HALO, span - 2 * HALO), :] = inner_ref[...]
        left_ref[pl.ds(span - HALO, HALO), :] = edge_ref[pl.ds(HALO, HALO), :]

    left = jnp.dot(left_ref[...], w_ref[b, :, : 2 * group], preferred_element_type=F32).astype(BF)
    own = own_ref[b]
    keys = jnp.concatenate([left[:, :group], own[:, :group]], axis=0)
    values = jnp.concatenate([left[:, group:], own[:, group : 2 * group]], axis=0)
    ctx = heads(own[:, 2 * group :], keys, values, bias_ref[...])
    settle(ctx, wout_ref, x_ref, gain_ref, valid_ref, x1_ref, g_ref, ctx_ref)


def attend(left_inner, left_edge, own, w, w_out, x, bias, gain, valid):
    blocks = w.shape[0]
    span, width = x.shape
    group = width // blocks
    return pl.pallas_call(
        attend_kernel,
        grid=(blocks,),
        out_shape=(
            jax.ShapeDtypeStruct((span, width), F32),
            jax.ShapeDtypeStruct((span, width), BF),
        ),
        in_specs=[
            whole(span - 2 * HALO, width),
            whole(2 * HALO, width),
            pl.BlockSpec(memory_space=pltpu.VMEM),
            pl.BlockSpec(memory_space=pltpu.VMEM),
            whole(width, width),
            whole(span, width),
            whole(2 * span, 128),
            whole(1, width),
            whole(span, 1),
        ],
        out_specs=(whole(span, width), whole(span, width)),
        scratch_shapes=[pltpu.VMEM((span, width), BF), pltpu.VMEM((span, width), BF)],
        compiler_params=params(),
        name="attend",
    )(left_inner, left_edge, in_vmem(own), in_vmem(w), in_hbm(w_out), x, bias, gain, valid)


def taps_over(pad_ref, taps, rows):
    y = jnp.zeros((rows, 128), F32)
    for r in range(8):
        hits = [(j, (j + 1) // 8) for j in range(KERNEL) if (j + 1) % 8 == r]
        deep = max(m for _, m in hits)
        moved = pad_ref[pl.ds(r, rows + 8 * deep), :]
        for j, m in hits:
            y = y + taps[j : j + 1, :] * moved[8 * m : 8 * m + rows]
    return y / (1.0 + jnp.exp(-y))


def inner_kernel(g_ref, x1_ref, taps_ref, valid_ref, gain_ref, x_ref, *rest):
    pad_ref = rest[-1]
    span, width = x1_ref.shape
    rows = pl.ds(HALO, span - 2 * HALO)
    for c in range(width // 128):
        cols = pl.ds(128 * c, 128)
        pad_ref[...] = g_ref[:, cols].astype(F32)
        silu = taps_over(pad_ref, taps_ref[:, cols], span - 2 * HALO)
        x_ref[:, cols] = ((x1_ref[rows, cols] + silu) * valid_ref[rows, :]).astype(BF)
    if len(rest) > 1:
        rest[0][...] = (normed(x_ref[...].astype(F32)) * gain_ref[...]).astype(BF)


def inner(g, x1, taps, valid, gain, last):
    span, width = x1.shape
    out = jax.ShapeDtypeStruct((span - 2 * HALO, width), BF)
    return pl.pallas_call(
        inner_kernel,
        out_shape=(out,) * (1 if last else 2),
        scratch_shapes=[pltpu.VMEM((span, 128), F32)],
        compiler_params=params(),
        name="inner",
    )(g, x1, taps, valid, gain)


def edges_kernel(count, g_ref, low_ref, high_ref, x1_ref, taps_ref, valid_ref, gain_ref, *rest):
    ins, outs, pad_ref = rest[:count], rest[count:-1], rest[-1]
    if count > 1:
        outs, edge_ref = outs[:-1], outs[-1]
    span, width = x1_ref.shape
    x_ref = outs[0]
    for at in (0, span - HALO):
        rows = pl.ds(at, HALO)
        for c in range(width // 128):
            cols = pl.ds(128 * c, 128)
            if at == 0:
                pad_ref[pl.ds(0, HALO), :] = low_ref[:, cols].astype(F32)
                pad_ref[pl.ds(HALO, 2 * HALO), :] = g_ref[pl.ds(0, 2 * HALO), cols].astype(F32)
            else:
                pad_ref[pl.ds(0, 2 * HALO), :] = g_ref[pl.ds(span - 2 * HALO, 2 * HALO), cols].astype(F32)
                pad_ref[pl.ds(2 * HALO, HALO), :] = high_ref[:, cols].astype(F32)
            silu = taps_over(pad_ref, taps_ref[:, cols], HALO)
            x_ref[rows, cols] = ((x1_ref[rows, cols] + silu) * valid_ref[rows, :]).astype(BF)
        if count > 1:
            h = (normed(x_ref[rows, :].astype(F32)) * gain_ref[...]).astype(BF)
            outs[1][rows, :] = h
            edge_ref[pl.ds(HALO if at else 0, HALO), :] = h
    rows = pl.ds(HALO, span - 2 * HALO)
    for source, target in zip(ins, outs):
        target[rows, :] = source[...]


def edges(g, low, high, x1, taps, valid, gain, inners):
    span, width = x1.shape
    count = len(inners)
    return pl.pallas_call(
        functools.partial(edges_kernel, count),
        out_shape=(jax.ShapeDtypeStruct((span, width), BF),) * count
        + (jax.ShapeDtypeStruct((2 * HALO, width), BF),) * (count - 1),
        scratch_shapes=[pltpu.VMEM((3 * HALO, 128), F32)],
        compiler_params=params(),
        name="edges",
    )(g, low, high, x1, taps, valid, gain, *inners)


def along(value, by):
    size = lax.axis_size(SEQ)
    pairs = [(i, i + by) for i in range(size) if 0 <= i + by < size]
    return lax.ppermute(value, SEQ, pairs)


def around(value, phase, by):
    ys = lax.axis_size("yh") * lax.axis_size("yl")
    xs, cores = lax.axis_size("x"), lax.axis_size("core")
    at = lambda y, x, core: ((y % ys) * xs + x % xs) * cores + core
    pairs = []
    for y in range(ys):
        for x in range(xs):
            for core in range(cores):
                along_x = (core == 0) == (phase == 1)
                to = at(y, x + by, core) if along_x else at(y + by, x, core)
                pairs.append((at(y, x, core), to))
    return lax.ppermute(value, ("yh", "yl", "x", "core"), pairs)


def weight_row(w, frames):
    rows, cols = w.shape
    zs, xs, yls, cores = (lax.axis_size(a) for a in ("z", "x", "yl", "core"))
    deep = rows // yls
    width = cols // 3
    group = width // xs
    at = lax.axis_index("yl") * deep
    col = lax.axis_index("x") * group
    own = jnp.concatenate(
        [lax.dynamic_slice(w, (at, part * width + col), (deep, group)) for part in (1, 2, 0)],
        axis=1,
    )
    half = zs // cores
    came = {}
    for k in range(1, half + 1):
        pairs = [(cores * z, cores * ((z + k) % zs)) for z in range(zs) if k < half]
        pairs += [(cores * z + 1, cores * ((z - k) % zs) + 1) for z in range(zs)]
        came[k] = lax.ppermute(own, ("z", "core"), pairs)
    first = lax.axis_index("core") == 0
    stack = jnp.concatenate(
        [
            jnp.where(first, came[k] if k else own, came[half - k])
            for k in range(half)
        ],
        axis=0,
    )
    stack, frames = lax.optimization_barrier((stack, frames))
    unit = stack.reshape(half, deep, 3 * group)
    before, after = around(unit, 1, 1), around(unit, 1, -1)
    far = [around(before[: half // 2], 1, 1), around(after[half // 2 :], 1, -1)]
    front = jnp.stack([unit, before])
    back = jnp.stack([after, jnp.concatenate(far, axis=0)])
    return front, back, frames


def swapped(values):
    return [lax.ppermute(v, "core", [(0, 1), (1, 0)]) for v in values]


def on_device(frames, arrival, lengths, attn_gain, w_qkv, w_out, conv_gain, conv_kernel):
    span = frames.shape[1]
    width = w_out.shape[0]
    group = lax.axis_index(DP)
    place = lax.axis_index(SEQ)
    groups = lax.axis_size(DP)
    front, back, frames = weight_row(w_qkv, frames)
    row_here = lax.dynamic_index_in_dim(arrival, place, 0, keepdims=False)
    chunks = frames.reshape(groups, span // groups, width)
    chunks = lax.all_to_all(chunks, DP, split_axis=0, concat_axis=0, tiled=True)
    chunks, front, back = lax.optimization_barrier((chunks, front, back))
    before = [around(front, 2, 1), around(back, 2, 1)]
    after = [around(front, 2, -1), around(back, 2, -1)]
    chunks = pick(chunks, row_here)
    chunks = lax.all_to_all(chunks, DP, split_axis=0, concat_axis=0, tiled=True)
    far = [around(before[0], 2, 1), around(after[1], 2, -1)]
    x = chunks.reshape(span, width)
    mine = [front, back] + before + after + far
    other = swapped(mine)

    length = lax.dynamic_index_in_dim(lengths, group, 0, keepdims=False)
    position = place * span + jnp.arange(span)
    own_valid = position < length
    left_valid = jnp.logical_and(position - span < length, place > 0)
    key_valid = jnp.concatenate([left_valid, own_valid])
    bias = jnp.where(key_valid, 0.0, -1e30).astype(BF)
    bias = jnp.where(jnp.arange(128)[None, :] == 0, bias[:, None], jnp.zeros((), BF))
    valid = own_valid.astype(F32)[:, None]
    gain_a = attn_gain[None, :]
    gain_c = conv_gain[None, :]
    taps = jnp.pad(conv_kernel, ((0, 1), (0, 0)))

    h, h_inner, edge = head(x, gain_a)
    left_inner = along(h_inner, 1)
    for step in range(ITERS):
        last = step == ITERS - 1
        left_edge = along(edge, 1)
        if step == 0:
            at = [lax.axis_index(a) for a in ("z", ("yh", "yl"), "x", "core")]
            w, own = opening(jnp.stack(at).astype(jnp.int32), h, mine, other)
        else:
            own = project(h, w)
        x1, g = attend(left_inner, left_edge, own, w, w_out, x, bias, gain_c, valid)
        low = along(g[span - HALO :], 1)
        high = along(g[:HALO], -1)
        inners = inner(g, x1, taps, valid, gain_a, last)
        if not last:
            h_inner, low, high = lax.optimization_barrier((inners[1], low, high))
            inners = (inners[0], h_inner)
            left_inner = along(h_inner, 1)
        out = edges(g, low, high, x1, taps, valid, gain_a, inners)
        x = out[0]
        if not last:
            h, edge = out[1:]
    return x[None]


def solution(mesh):
    fine = Mesh(mesh.devices.reshape(8, 2, 2, 4, 2), DP + SEQ)
    placed = (P(DP, SEQ, None), P(), P(), P(), P(DP, None), P(), P(), P())
    return jax.shard_map(
        on_device, mesh=fine, in_specs=placed, out_specs=P(DP, SEQ, None), check_vma=False
    )
```

```python
import functools

import jax
import jax.numpy as jnp
from jax import lax
from jax.experimental import pallas as pl
from jax.experimental.pallas import tpu as pltpu
from jax.sharding import Mesh, PartitionSpec as P

HEAD = 64
KERNEL = 31
ITERS = 2
HALO = 16
EPS = 1e-05
DP = ("z", "yh")
SEQ = ("yl", "x", "core")
BF = jnp.bfloat16
F32 = jnp.float32
VMEM = 24 * 1024 * 1024


def params(**kw):
    return pltpu.CompilerParams(vmem_limit_bytes=VMEM, **kw)


def in_vmem(v):
    return pltpu.with_memory_space_constraint(v, pltpu.VMEM)


def in_hbm(v):
    return pltpu.with_memory_space_constraint(v, pltpu.HBM)


def normed(v):
    mean = jnp.mean(v, axis=-1, keepdims=True)
    d = v - mean
    var = jnp.mean(d * d, axis=-1, keepdims=True)
    return d * lax.rsqrt(var + EPS)


def pick_kernel(row_ref, in_ref, out_ref):
    for r in range(in_ref.shape[0]):
        out_ref[r] = in_ref[row_ref[r]]


def pick(chunks, row):
    return pl.pallas_call(
        pick_kernel,
        out_shape=jax.ShapeDtypeStruct(chunks.shape, chunks.dtype),
        in_specs=[
            pl.BlockSpec(memory_space=pltpu.SMEM),
            pl.BlockSpec(memory_space=pltpu.VMEM),
        ],
        out_specs=pl.BlockSpec(memory_space=pltpu.VMEM),
        compiler_params=params(),
        name="pick",
    )(row, chunks)


def head_kernel(x_ref, gain_ref, out_ref):
    out_ref[...] = (normed(x_ref[...].astype(F32)) * gain_ref[...]).astype(BF)


def head(x, gain):
    return pl.pallas_call(
        head_kernel,
        out_shape=jax.ShapeDtypeStruct(x.shape, BF),
        compiler_params=params(),
        name="head",
    )(x, gain)


def project_kernel(h_ref, w_ref, out_ref):
    for b in range(w_ref.shape[0]):
        out_ref[b] = jnp.dot(h_ref[...], w_ref[b], preferred_element_type=F32).astype(BF)


def project(h, w):
    blocks, _, cols = w.shape
    return pl.pallas_call(
        project_kernel,
        out_shape=pltpu.VMEM((blocks, h.shape[0], cols), BF),
        compiler_params=params(),
        name="project",
    )(h, in_vmem(w))


def heads(query, keys, values, bias):
    span = query.shape[0]
    lane = lax.broadcasted_iota(jnp.int32, (span, 128), 1)
    low = lane < HEAD
    tag = jnp.where(lane == 0, 1.0, 0.0).astype(BF)
    ones = jnp.ones((2 * span, 128), BF)
    outs = []
    for at in range(0, query.shape[1], 128):
        k = jnp.concatenate([keys[:, at : at + 128], bias], axis=1)
        v = jnp.concatenate([values[:, at : at + 128], ones], axis=1)
        q = query[:, at : at + 128] * jnp.asarray(HEAD ** (-0.5), BF)
        halves = []
        for mask in (low, jnp.logical_not(low)):
            qh = jnp.concatenate([jnp.where(mask, q, jnp.zeros_like(q)), tag], axis=1)
            s = lax.dot_general(qh, k, (((1,), (1,)), ((), ())), preferred_element_type=F32)
            top = jnp.max(s, axis=-1, keepdims=True)
            e = jnp.exp(s - top).astype(BF)
            o = jnp.dot(e, v, preferred_element_type=F32)
            halves.append(o[:, :128] / o[:, 128:])
        outs.append(jnp.where(low, halves[0], halves[1]).astype(BF))
    return jnp.concatenate(outs, axis=1)


def settle(ctx, wout_ref, x_ref, gain_ref, valid_ref, x1_ref, g_ref, ctx_ref):
    b = pl.program_id(0)
    group = ctx.shape[1]
    ctx_ref[:, pl.ds(pl.multiple_of(b * group, group), group)] = ctx

    @pl.when(b == pl.num_programs(0) - 1)
    def _():
        x1 = x_ref[...].astype(F32) + jnp.dot(
            ctx_ref[...], wout_ref[...], preferred_element_type=F32
        )
        x1_ref[...] = x1
        g_ref[...] = (normed(x1) * gain_ref[...] * valid_ref[...]).astype(BF)


OFFSETS = (0, 3, 1, 2)


def opening_kernel(at_ref, h_ref, *refs):
    mine, other = refs[:8], refs[8:16]
    wall_ref, out_ref, sem = refs[16:]
    blocks = wall_ref.shape[0]
    half, rows = mine[0].shape[1:3]
    z, y, x, core = (at_ref[i] for i in range(4))

    def unit(held, j, u):
        return held[2 * j + u // 2].at[u % 2]

    def fetch(b):
        block = lax.rem(x + OFFSETS[b], blocks)
        for lane in range(2):
            for held, here in ((mine, core == lane), (other, core != lane)):

                @pl.when(here)
                def _():
                    for k in range(len(OFFSETS)):
                        source = unit(held, b, k) if lane else unit(held, k, b)
                        part = lax.rem(y + OFFSETS[k], len(OFFSETS))
                        for slot in range(half):
                            to = lax.rem(z + 2 * half - (lane * half + slot), 2 * half)
                            row = pl.multiple_of((to * len(OFFSETS) + part) * rows, rows)
                            pltpu.make_async_copy(
                                source.at[slot], wall_ref.at[block, pl.ds(row, rows)], sem.at[b]
                            ).start()

    fetch(0)
    for b in range(blocks):
        if b + 1 < blocks:
            fetch(b + 1)
        block = lax.rem(x + OFFSETS[b], blocks)
        pltpu.make_async_copy(wall_ref.at[block], wall_ref.at[block], sem.at[b]).wait()
        out_ref[block] = jnp.dot(
            h_ref[...], wall_ref[block], preferred_element_type=F32
        ).astype(BF)


def opening(at, h, mine, other):
    _, half, rows, cols = mine[0].shape
    depth = 2 * half * len(OFFSETS) * rows
    blocks = len(OFFSETS)
    space = pl.BlockSpec(memory_space=pltpu.VMEM)
    anywhere = pl.BlockSpec(memory_space=pl.ANY)
    return pl.pallas_call(
        opening_kernel,
        out_shape=(
            pltpu.VMEM((blocks, depth, cols), BF),
            pltpu.VMEM((blocks, h.shape[0], cols), BF),
        ),
        in_specs=[pl.BlockSpec(memory_space=pltpu.SMEM), space] + [anywhere] * 16,
        out_specs=(space, space),
        scratch_shapes=[pltpu.SemaphoreType.DMA((blocks,))],
        compiler_params=params(),
        name="opening",
    )(at, h, *(in_hbm(v) for v in (*mine, *other)))


def whole(*shape):
    return pl.BlockSpec(shape, lambda b: (0,) * len(shape))


def attend_kernel(count, *refs):
    came = refs[:count]
    own_ref, w_ref, wout_ref, x_ref, bias_ref, gain_ref, valid_ref = refs[count : count + 7]
    x1_ref, g_ref, ctx_ref, left_ref = refs[count + 7 :]
    b = pl.program_id(0)
    group = wout_ref.shape[0] // w_ref.shape[0]
    span = left_ref.shape[0]

    @pl.when(b == 0)
    def _():
        if count == 1:
            left_ref[...] = came[0][...]
        else:
            inner_ref, edge_ref = came
            left_ref[pl.ds(0, HALO), :] = edge_ref[pl.ds(0, HALO), :]
            left_ref[pl.ds(HALO, span - 2 * HALO), :] = inner_ref[...]
            left_ref[pl.ds(span - HALO, HALO), :] = edge_ref[pl.ds(HALO, HALO), :]

    left = jnp.dot(left_ref[...], w_ref[b, :, : 2 * group], preferred_element_type=F32).astype(BF)
    own = own_ref[b]
    keys = jnp.concatenate([left[:, :group], own[:, :group]], axis=0)
    values = jnp.concatenate([left[:, group:], own[:, group : 2 * group]], axis=0)
    ctx = heads(own[:, 2 * group :], keys, values, bias_ref[...])
    settle(ctx, wout_ref, x_ref, gain_ref, valid_ref, x1_ref, g_ref, ctx_ref)


def attend(left, own, w, w_out, x, bias, gain, valid):
    blocks = w.shape[0]
    span, width = x.shape
    group = width // blocks
    return pl.pallas_call(
        functools.partial(attend_kernel, len(left)),
        grid=(blocks,),
        out_shape=(
            jax.ShapeDtypeStruct((span, width), F32),
            jax.ShapeDtypeStruct((span, width), BF),
        ),
        in_specs=[
            *(whole(*v.shape) for v in left),
            pl.BlockSpec(memory_space=pltpu.VMEM),
            pl.BlockSpec(memory_space=pltpu.VMEM),
            whole(width, width),
            whole(span, width),
            whole(2 * span, 128),
            whole(1, width),
            whole(span, 1),
        ],
        out_specs=(whole(span, width), whole(span, width)),
        scratch_shapes=[pltpu.VMEM((span, width), BF), pltpu.VMEM((span, width), BF)],
        compiler_params=params(),
        name="attend",
    )(*left, in_vmem(own), in_vmem(w), in_hbm(w_out), x, bias, gain, valid)


def taps_over(pad_ref, taps, rows):
    y = jnp.zeros((rows, 128), F32)
    for r in range(8):
        hits = [(j, (j + 1) // 8) for j in range(KERNEL) if (j + 1) % 8 == r]
        deep = max(m for _, m in hits)
        moved = pad_ref[pl.ds(r, rows + 8 * deep), :]
        for j, m in hits:
            y = y + taps[j : j + 1, :] * moved[8 * m : 8 * m + rows]
    return y / (1.0 + jnp.exp(-y))


def inner_kernel(g_ref, x1_ref, taps_ref, valid_ref, gain_ref, x_ref, *rest):
    pad_ref = rest[-1]
    span, width = x1_ref.shape
    rows = pl.ds(HALO, span - 2 * HALO)
    for c in range(width // 128):
        cols = pl.ds(128 * c, 128)
        pad_ref[...] = g_ref[:, cols].astype(F32)
        silu = taps_over(pad_ref, taps_ref[:, cols], span - 2 * HALO)
        x_ref[:, cols] = ((x1_ref[rows, cols] + silu) * valid_ref[rows, :]).astype(BF)
    if len(rest) > 1:
        rest[0][...] = (normed(x_ref[...].astype(F32)) * gain_ref[...]).astype(BF)


def inner(g, x1, taps, valid, gain, last):
    span, width = x1.shape
    out = jax.ShapeDtypeStruct((span - 2 * HALO, width), BF)
    return pl.pallas_call(
        inner_kernel,
        out_shape=(out,) * (1 if last else 2),
        scratch_shapes=[pltpu.VMEM((span, 128), F32)],
        compiler_params=params(),
        name="inner",
    )(g, x1, taps, valid, gain)


def edges_kernel(count, g_ref, low_ref, high_ref, x1_ref, taps_ref, valid_ref, gain_ref, *rest):
    ins, outs, pad_ref = rest[:count], rest[count:-1], rest[-1]
    if count > 1:
        outs, edge_ref = outs[:-1], outs[-1]
    span, width = x1_ref.shape
    x_ref = outs[0]
    for at in (0, span - HALO):
        rows = pl.ds(at, HALO)
        for c in range(width // 128):
            cols = pl.ds(128 * c, 128)
            if at == 0:
                pad_ref[pl.ds(0, HALO), :] = low_ref[:, cols].astype(F32)
                pad_ref[pl.ds(HALO, 2 * HALO), :] = g_ref[pl.ds(0, 2 * HALO), cols].astype(F32)
            else:
                pad_ref[pl.ds(0, 2 * HALO), :] = g_ref[pl.ds(span - 2 * HALO, 2 * HALO), cols].astype(F32)
                pad_ref[pl.ds(2 * HALO, HALO), :] = high_ref[:, cols].astype(F32)
            silu = taps_over(pad_ref, taps_ref[:, cols], HALO)
            x_ref[rows, cols] = ((x1_ref[rows, cols] + silu) * valid_ref[rows, :]).astype(BF)
        if count > 1:
            h = (normed(x_ref[rows, :].astype(F32)) * gain_ref[...]).astype(BF)
            outs[1][rows, :] = h
            edge_ref[pl.ds(HALO if at else 0, HALO), :] = h
    rows = pl.ds(HALO, span - 2 * HALO)
    for source, target in zip(ins, outs):
        target[rows, :] = source[...]


def edges(g, low, high, x1, taps, valid, gain, inners):
    span, width = x1.shape
    count = len(inners)
    return pl.pallas_call(
        functools.partial(edges_kernel, count),
        out_shape=(jax.ShapeDtypeStruct((span, width), BF),) * count
        + (jax.ShapeDtypeStruct((2 * HALO, width), BF),) * (count - 1),
        scratch_shapes=[pltpu.VMEM((3 * HALO, 128), F32)],
        compiler_params=params(),
        name="edges",
    )(g, low, high, x1, taps, valid, gain, *inners)


def along(value, by):
    size = lax.axis_size(SEQ)
    pairs = [(i, i + by) for i in range(size) if 0 <= i + by < size]
    return lax.ppermute(value, SEQ, pairs)


def around(value, phase, by):
    ys = lax.axis_size("yh") * lax.axis_size("yl")
    xs, cores = lax.axis_size("x"), lax.axis_size("core")
    at = lambda y, x, core: ((y % ys) * xs + x % xs) * cores + core
    pairs = []
    for y in range(ys):
        for x in range(xs):
            for core in range(cores):
                along_x = (core == 0) == (phase == 1)
                to = at(y, x + by, core) if along_x else at(y + by, x, core)
                pairs.append((at(y, x, core), to))
    return lax.ppermute(value, ("yh", "yl", "x", "core"), pairs)


def weight_row(w):
    rows, cols = w.shape
    zs, xs, yls, cores = (lax.axis_size(a) for a in ("z", "x", "yl", "core"))
    deep = rows // yls
    width = cols // 3
    group = width // xs
    at = lax.axis_index("yl") * deep
    col = lax.axis_index("x") * group
    own = jnp.concatenate(
        [lax.dynamic_slice(w, (at, part * width + col), (deep, group)) for part in (1, 2, 0)],
        axis=1,
    )
    half = zs // cores
    came = {}
    for k in range(1, half + 1):
        pairs = [(cores * z, cores * ((z + k) % zs)) for z in range(zs) if k < half]
        pairs += [(cores * z + 1, cores * ((z - k) % zs) + 1) for z in range(zs)]
        came[k] = lax.ppermute(own, ("z", "core"), pairs)
    first = lax.axis_index("core") == 0
    stack = jnp.concatenate(
        [
            jnp.where(first, came[k] if k else own, came[half - k])
            for k in range(half)
        ],
        axis=0,
    )
    unit = stack.reshape(half, deep, 3 * group)
    before, after = around(unit, 1, 1), around(unit, 1, -1)
    far = [around(before[: half // 2], 1, 1), around(after[half // 2 :], 1, -1)]
    front = jnp.stack([unit, before])
    back = jnp.stack([after, jnp.concatenate(far, axis=0)])
    return front, back


def swapped(values):
    return [lax.ppermute(v, "core", [(0, 1), (1, 0)]) for v in values]


def on_device(frames, arrival, lengths, attn_gain, w_qkv, w_out, conv_gain, conv_kernel):
    span = frames.shape[1]
    width = w_out.shape[0]
    group = lax.axis_index(DP)
    place = lax.axis_index(SEQ)
    groups = lax.axis_size(DP)
    front, back = weight_row(w_qkv)
    row_here = lax.dynamic_index_in_dim(arrival, place, 0, keepdims=False)
    chunks = frames.reshape(groups, span // groups, width)
    chunks = lax.all_to_all(chunks, DP, split_axis=0, concat_axis=0, tiled=True)
    chunks, front, back = lax.optimization_barrier((chunks, front, back))
    before = [around(front, 2, 1), around(back, 2, 1)]
    after = [around(front, 2, -1), around(back, 2, -1)]
    chunks = pick(chunks, row_here)
    chunks = lax.all_to_all(chunks, DP, split_axis=0, concat_axis=0, tiled=True)
    far = [around(before[0], 2, 1), around(after[1], 2, -1)]
    x = chunks.reshape(span, width)
    mine = [front, back] + before + after + far
    other = swapped(mine)

    length = lax.dynamic_index_in_dim(lengths, group, 0, keepdims=False)
    position = place * span + jnp.arange(span)
    own_valid = position < length
    left_valid = jnp.logical_and(position - span < length, place > 0)
    key_valid = jnp.concatenate([left_valid, own_valid])
    bias = jnp.where(key_valid, 0.0, -1e30).astype(BF)
    bias = jnp.where(jnp.arange(128)[None, :] == 0, bias[:, None], jnp.zeros((), BF))
    valid = own_valid.astype(F32)[:, None]
    gain_a = attn_gain[None, :]
    gain_c = conv_gain[None, :]
    taps = jnp.pad(conv_kernel, ((0, 1), (0, 0)))

    h = head(x, gain_a)
    left = [along(h, 1)]
    for step in range(ITERS):
        last = step == ITERS - 1
        if step == 0:
            at = [lax.axis_index(a) for a in ("z", ("yh", "yl"), "x", "core")]
            w, own = opening(jnp.stack(at).astype(jnp.int32), h, mine, other)
        else:
            own = project(h, w)
        x1, g = attend(left, own, w, w_out, x, bias, gain_c, valid)
        low = along(g[span - HALO :], 1)
        high = along(g[:HALO], -1)
        inners = inner(g, x1, taps, valid, gain_a, last)
        if not last:
            h_inner, low, high = lax.optimization_barrier((inners[1], low, high))
            inners = (inners[0], h_inner)
            left = [along(h_inner, 1)]
        out = edges(g, low, high, x1, taps, valid, gain_a, inners)
        x = out[0]
        if not last:
            h, edge = out[1:]
            left.append(along(edge, 1))
    return x[None]


def solution(mesh):
    fine = Mesh(mesh.devices.reshape(8, 2, 2, 4, 2), DP + SEQ)
    placed = (P(DP, SEQ, None), P(), P(), P(), P(DP, None), P(), P(), P())
    return jax.shard_map(
        on_device, mesh=fine, in_specs=placed, out_specs=P(DP, SEQ, None), check_vma=False
    )
```

```python
import functools

import jax
import jax.numpy as jnp
from jax import lax
from jax.experimental import pallas as pl
from jax.experimental.pallas import tpu as pltpu
from jax.sharding import Mesh, PartitionSpec as P

HEAD = 64
KERNEL = 31
ITERS = 2
HALO = 16
EPS = 1e-05
DP = ("z", "yh")
SEQ = ("yl", "x", "core")
BF = jnp.bfloat16
F32 = jnp.float32
VMEM = 24 * 1024 * 1024


def params(**kw):
    return pltpu.CompilerParams(vmem_limit_bytes=VMEM, **kw)


def in_vmem(v):
    return pltpu.with_memory_space_constraint(v, pltpu.VMEM)


def in_hbm(v):
    return pltpu.with_memory_space_constraint(v, pltpu.HBM)


def normed(v):
    mean = jnp.mean(v, axis=-1, keepdims=True)
    d = v - mean
    var = jnp.mean(d * d, axis=-1, keepdims=True)
    return d * lax.rsqrt(var + EPS)


def pick_kernel(row_ref, in_ref, out_ref):
    for r in range(in_ref.shape[0]):
        out_ref[r] = in_ref[row_ref[r]]


def pick(chunks, row):
    return pl.pallas_call(
        pick_kernel,
        out_shape=jax.ShapeDtypeStruct(chunks.shape, chunks.dtype),
        in_specs=[
            pl.BlockSpec(memory_space=pltpu.SMEM),
            pl.BlockSpec(memory_space=pltpu.VMEM),
        ],
        out_specs=pl.BlockSpec(memory_space=pltpu.VMEM),
        compiler_params=params(),
        name="pick",
    )(row, chunks)


def head_kernel(x_ref, gain_ref, out_ref):
    out_ref[...] = (normed(x_ref[...].astype(F32)) * gain_ref[...]).astype(BF)


def head(x, gain):
    return pl.pallas_call(
        head_kernel,
        out_shape=jax.ShapeDtypeStruct(x.shape, BF),
        compiler_params=params(),
        name="head",
    )(x, gain)


def project_kernel(h_ref, w_ref, out_ref):
    for b in range(w_ref.shape[0]):
        out_ref[b] = jnp.dot(h_ref[...], w_ref[b], preferred_element_type=F32).astype(BF)


def project(h, w):
    blocks, _, cols = w.shape
    return pl.pallas_call(
        project_kernel,
        out_shape=pltpu.VMEM((blocks, h.shape[0], cols), BF),
        compiler_params=params(),
        name="project",
    )(h, in_vmem(w))


def heads(query, keys, values, bias):
    span = query.shape[0]
    lane = lax.broadcasted_iota(jnp.int32, (span, 128), 1)
    low = lane < HEAD
    tag = jnp.where(lane == 0, 1.0, 0.0).astype(BF)
    ones = jnp.ones((2 * span, 128), BF)
    outs = []
    for at in range(0, query.shape[1], 128):
        k = jnp.concatenate([keys[:, at : at + 128], bias], axis=1)
        v = jnp.concatenate([values[:, at : at + 128], ones], axis=1)
        q = query[:, at : at + 128] * jnp.asarray(HEAD ** (-0.5), BF)
        halves = []
        for mask in (low, jnp.logical_not(low)):
            qh = jnp.concatenate([jnp.where(mask, q, jnp.zeros_like(q)), tag], axis=1)
            s = lax.dot_general(qh, k, (((1,), (1,)), ((), ())), preferred_element_type=F32)
            top = jnp.max(s, axis=-1, keepdims=True)
            e = jnp.exp(s - top).astype(BF)
            o = jnp.dot(e, v, preferred_element_type=F32)
            halves.append(o[:, :128] / o[:, 128:])
        outs.append(jnp.where(low, halves[0], halves[1]).astype(BF))
    return jnp.concatenate(outs, axis=1)


def settle(ctx, fetch, wout_ref, x_ref, gain_ref, valid_ref, x1_ref, g_ref, ctx_ref):
    b = pl.program_id(0)
    group = ctx.shape[1]
    ctx_ref[:, pl.ds(pl.multiple_of(b * group, group), group)] = ctx

    @pl.when(b == pl.num_programs(0) - 1)
    def _():
        fetch.wait()
        x1 = x_ref[...].astype(F32) + jnp.dot(
            ctx_ref[...], wout_ref[...], preferred_element_type=F32
        )
        x1_ref[...] = x1
        g_ref[...] = (normed(x1) * gain_ref[...] * valid_ref[...]).astype(BF)


OFFSETS = (0, 3, 1, 2)


def opening_kernel(at_ref, h_ref, *refs):
    mine, other = refs[:8], refs[8:16]
    wall_ref, out_ref, sem = refs[16:]
    blocks = wall_ref.shape[0]
    half, rows = mine[0].shape[1:3]
    z, y, x, core = (at_ref[i] for i in range(4))

    def unit(held, j, u):
        return held[2 * j + u // 2].at[u % 2]

    def fetch(b):
        block = lax.rem(x + OFFSETS[b], blocks)
        for lane in range(2):
            for held, here in ((mine, core == lane), (other, core != lane)):

                @pl.when(here)
                def _():
                    for k in range(len(OFFSETS)):
                        source = unit(held, b, k) if lane else unit(held, k, b)
                        part = lax.rem(y + OFFSETS[k], len(OFFSETS))
                        for slot in range(half):
                            to = lax.rem(z + 2 * half - (lane * half + slot), 2 * half)
                            row = pl.multiple_of((to * len(OFFSETS) + part) * rows, rows)
                            pltpu.make_async_copy(
                                source.at[slot], wall_ref.at[block, pl.ds(row, rows)], sem.at[b]
                            ).start()

    fetch(0)
    for b in range(blocks):
        if b + 1 < blocks:
            fetch(b + 1)
        block = lax.rem(x + OFFSETS[b], blocks)
        pltpu.make_async_copy(wall_ref.at[block], wall_ref.at[block], sem.at[b]).wait()
        out_ref[block] = jnp.dot(
            h_ref[...], wall_ref[block], preferred_element_type=F32
        ).astype(BF)


def opening(at, h, mine, other):
    _, half, rows, cols = mine[0].shape
    depth = 2 * half * len(OFFSETS) * rows
    blocks = len(OFFSETS)
    space = pl.BlockSpec(memory_space=pltpu.VMEM)
    anywhere = pl.BlockSpec(memory_space=pl.ANY)
    return pl.pallas_call(
        opening_kernel,
        out_shape=(
            pltpu.VMEM((blocks, depth, cols), BF),
            pltpu.VMEM((blocks, h.shape[0], cols), BF),
        ),
        in_specs=[pl.BlockSpec(memory_space=pltpu.SMEM), space] + [anywhere] * 16,
        out_specs=(space, space),
        scratch_shapes=[pltpu.SemaphoreType.DMA((blocks,))],
        compiler_params=params(),
        name="opening",
    )(at, h, *(in_hbm(v) for v in (*mine, *other)))


def whole(*shape):
    return pl.BlockSpec(shape, lambda b: (0,) * len(shape))


def attend_kernel(count, *refs):
    came = refs[:count]
    own_ref, w_ref, wout_ref, x_ref, bias_ref, gain_ref, valid_ref = refs[count : count + 7]
    x1_ref, g_ref, ctx_ref, left_ref, held_ref, sem = refs[count + 7 :]
    fetch = pltpu.make_async_copy(wout_ref, held_ref, sem)
    b = pl.program_id(0)
    group = wout_ref.shape[0] // w_ref.shape[0]
    span = left_ref.shape[0]

    @pl.when(b == 0)
    def _():
        fetch.start()
        if count == 1:
            left_ref[...] = came[0][...]
        else:
            inner_ref, edge_ref = came
            left_ref[pl.ds(0, HALO), :] = edge_ref[pl.ds(0, HALO), :]
            left_ref[pl.ds(HALO, span - 2 * HALO), :] = inner_ref[...]
            left_ref[pl.ds(span - HALO, HALO), :] = edge_ref[pl.ds(HALO, HALO), :]

    left = jnp.dot(left_ref[...], w_ref[b, :, : 2 * group], preferred_element_type=F32).astype(BF)
    own = own_ref[b]
    keys = jnp.concatenate([left[:, :group], own[:, :group]], axis=0)
    values = jnp.concatenate([left[:, group:], own[:, group : 2 * group]], axis=0)
    ctx = heads(own[:, 2 * group :], keys, values, bias_ref[...])
    settle(ctx, fetch, held_ref, x_ref, gain_ref, valid_ref, x1_ref, g_ref, ctx_ref)


def attend(left, own, w, w_out, x, bias, gain, valid):
    blocks = w.shape[0]
    span, width = x.shape
    group = width // blocks
    return pl.pallas_call(
        functools.partial(attend_kernel, len(left)),
        grid=(blocks,),
        out_shape=(
            jax.ShapeDtypeStruct((span, width), F32),
            jax.ShapeDtypeStruct((span, width), BF),
        ),
        in_specs=[
            *(whole(*v.shape) for v in left),
            pl.BlockSpec(memory_space=pltpu.VMEM),
            pl.BlockSpec(memory_space=pltpu.VMEM),
            pl.BlockSpec(memory_space=pl.ANY),
            whole(span, width),
            whole(2 * span, 128),
            whole(1, width),
            whole(span, 1),
        ],
        out_specs=(whole(span, width), whole(span, width)),
        scratch_shapes=[
            pltpu.VMEM((span, width), BF),
            pltpu.VMEM((span, width), BF),
            pltpu.VMEM((width, width), BF),
            pltpu.SemaphoreType.DMA(()),
        ],
        compiler_params=params(),
        name="attend",
    )(*left, in_vmem(own), in_vmem(w), in_hbm(w_out), x, bias, gain, valid)


def taps_over(pad_ref, taps, rows):
    y = jnp.zeros((rows, 128), F32)
    for r in range(8):
        hits = [(j, (j + 1) // 8) for j in range(KERNEL) if (j + 1) % 8 == r]
        deep = max(m for _, m in hits)
        moved = pad_ref[pl.ds(r, rows + 8 * deep), :]
        for j, m in hits:
            y = y + taps[j : j + 1, :] * moved[8 * m : 8 * m + rows]
    return y / (1.0 + jnp.exp(-y))


def inner_kernel(g_ref, x1_ref, taps_ref, valid_ref, gain_ref, x_ref, *rest):
    pad_ref = rest[-1]
    span, width = x1_ref.shape
    rows = pl.ds(HALO, span - 2 * HALO)
    for c in range(width // 128):
        cols = pl.ds(128 * c, 128)
        pad_ref[...] = g_ref[:, cols].astype(F32)
        silu = taps_over(pad_ref, taps_ref[:, cols], span - 2 * HALO)
        x_ref[:, cols] = ((x1_ref[rows, cols] + silu) * valid_ref[rows, :]).astype(BF)
    if len(rest) > 1:
        rest[0][...] = (normed(x_ref[...].astype(F32)) * gain_ref[...]).astype(BF)


def inner(g, x1, taps, valid, gain, last):
    span, width = x1.shape
    out = jax.ShapeDtypeStruct((span - 2 * HALO, width), BF)
    return pl.pallas_call(
        inner_kernel,
        out_shape=(out,) * (1 if last else 2),
        scratch_shapes=[pltpu.VMEM((span, 128), F32)],
        compiler_params=params(),
        name="inner",
    )(g, x1, taps, valid, gain)


def edges_kernel(count, g_ref, low_ref, high_ref, x1_ref, taps_ref, valid_ref, gain_ref, *rest):
    ins, outs, pad_ref = rest[:count], rest[count:-1], rest[-1]
    if count > 1:
        outs, edge_ref = outs[:-1], outs[-1]
    span, width = x1_ref.shape
    x_ref = outs[0]
    for at in (0, span - HALO):
        rows = pl.ds(at, HALO)
        for c in range(width // 128):
            cols = pl.ds(128 * c, 128)
            if at == 0:
                pad_ref[pl.ds(0, HALO), :] = low_ref[:, cols].astype(F32)
                pad_ref[pl.ds(HALO, 2 * HALO), :] = g_ref[pl.ds(0, 2 * HALO), cols].astype(F32)
            else:
                pad_ref[pl.ds(0, 2 * HALO), :] = g_ref[pl.ds(span - 2 * HALO, 2 * HALO), cols].astype(F32)
                pad_ref[pl.ds(2 * HALO, HALO), :] = high_ref[:, cols].astype(F32)
            silu = taps_over(pad_ref, taps_ref[:, cols], HALO)
            x_ref[rows, cols] = ((x1_ref[rows, cols] + silu) * valid_ref[rows, :]).astype(BF)
        if count > 1:
            h = (normed(x_ref[rows, :].astype(F32)) * gain_ref[...]).astype(BF)
            outs[1][rows, :] = h
            edge_ref[pl.ds(HALO if at else 0, HALO), :] = h
    rows = pl.ds(HALO, span - 2 * HALO)
    for source, target in zip(ins, outs):
        target[rows, :] = source[...]


def edges(g, low, high, x1, taps, valid, gain, inners):
    span, width = x1.shape
    count = len(inners)
    return pl.pallas_call(
        functools.partial(edges_kernel, count),
        out_shape=(jax.ShapeDtypeStruct((span, width), BF),) * count
        + (jax.ShapeDtypeStruct((2 * HALO, width), BF),) * (count - 1),
        scratch_shapes=[pltpu.VMEM((3 * HALO, 128), F32)],
        compiler_params=params(),
        name="edges",
    )(g, low, high, x1, taps, valid, gain, *inners)


def along(value, by):
    size = lax.axis_size(SEQ)
    pairs = [(i, i + by) for i in range(size) if 0 <= i + by < size]
    return lax.ppermute(value, SEQ, pairs)


def around(value, phase, by):
    ys = lax.axis_size("yh") * lax.axis_size("yl")
    xs, cores = lax.axis_size("x"), lax.axis_size("core")
    at = lambda y, x, core: ((y % ys) * xs + x % xs) * cores + core
    pairs = []
    for y in range(ys):
        for x in range(xs):
            for core in range(cores):
                along_x = (core == 0) == (phase == 1)
                to = at(y, x + by, core) if along_x else at(y + by, x, core)
                pairs.append((at(y, x, core), to))
    return lax.ppermute(value, ("yh", "yl", "x", "core"), pairs)


def weight_row(w):
    rows, cols = w.shape
    zs, xs, yls, cores = (lax.axis_size(a) for a in ("z", "x", "yl", "core"))
    deep = rows // yls
    width = cols // 3
    group = width // xs
    at = lax.axis_index("yl") * deep
    col = lax.axis_index("x") * group
    own = jnp.concatenate(
        [lax.dynamic_slice(w, (at, part * width + col), (deep, group)) for part in (1, 2, 0)],
        axis=1,
    )
    half = zs // cores
    came = {}
    for k in range(1, half + 1):
        pairs = [(cores * z, cores * ((z + k) % zs)) for z in range(zs) if k < half]
        pairs += [(cores * z + 1, cores * ((z - k) % zs) + 1) for z in range(zs)]
        came[k] = lax.ppermute(own, ("z", "core"), pairs)
    first = lax.axis_index("core") == 0
    stack = jnp.concatenate(
        [
            jnp.where(first, came[k] if k else own, came[half - k])
            for k in range(half)
        ],
        axis=0,
    )
    unit = stack.reshape(half, deep, 3 * group)
    before, after = around(unit, 1, 1), around(unit, 1, -1)
    far = [around(before[: half // 2], 1, 1), around(after[half // 2 :], 1, -1)]
    front = jnp.stack([unit, before])
    back = jnp.stack([after, jnp.concatenate(far, axis=0)])
    return front, back


def swapped(values):
    return [lax.ppermute(v, "core", [(0, 1), (1, 0)]) for v in values]


def on_device(frames, arrival, lengths, attn_gain, w_qkv, w_out, conv_gain, conv_kernel):
    span = frames.shape[1]
    width = w_out.shape[0]
    group = lax.axis_index(DP)
    place = lax.axis_index(SEQ)
    groups = lax.axis_size(DP)
    front, back = weight_row(w_qkv)
    row_here = lax.dynamic_index_in_dim(arrival, place, 0, keepdims=False)
    chunks = frames.reshape(groups, span // groups, width)
    chunks = lax.all_to_all(chunks, DP, split_axis=0, concat_axis=0, tiled=True)
    chunks, front, back = lax.optimization_barrier((chunks, front, back))
    before = [around(front, 2, 1), around(back, 2, 1)]
    after = [around(front, 2, -1), around(back, 2, -1)]
    chunks = pick(chunks, row_here)
    chunks = lax.all_to_all(chunks, DP, split_axis=0, concat_axis=0, tiled=True)
    far = [around(before[0], 2, 1), around(after[1], 2, -1)]
    x = chunks.reshape(span, width)
    mine = [front, back] + before + after + far
    other = swapped(mine)

    length = lax.dynamic_index_in_dim(lengths, group, 0, keepdims=False)
    position = place * span + jnp.arange(span)
    own_valid = position < length
    left_valid = jnp.logical_and(position - span < length, place > 0)
    key_valid = jnp.concatenate([left_valid, own_valid])
    bias = jnp.where(key_valid, 0.0, -1e30).astype(BF)
    bias = jnp.where(jnp.arange(128)[None, :] == 0, bias[:, None], jnp.zeros((), BF))
    valid = own_valid.astype(F32)[:, None]
    gain_a = attn_gain[None, :]
    gain_c = conv_gain[None, :]
    taps = jnp.pad(conv_kernel, ((0, 1), (0, 0)))

    h = head(x, gain_a)
    left = [along(h, 1)]
    for step in range(ITERS):
        last = step == ITERS - 1
        if step == 0:
            at = [lax.axis_index(a) for a in ("z", ("yh", "yl"), "x", "core")]
            w, own = opening(jnp.stack(at).astype(jnp.int32), h, mine, other)
        else:
            own = project(h, w)
        x1, g = attend(left, own, w, w_out, x, bias, gain_c, valid)
        low = along(g[span - HALO :], 1)
        high = along(g[:HALO], -1)
        inners = inner(g, x1, taps, valid, gain_a, last)
        if not last:
            h_inner, low, high = lax.optimization_barrier((inners[1], low, high))
            inners = (inners[0], h_inner)
            left = [along(h_inner, 1)]
        out = edges(g, low, high, x1, taps, valid, gain_a, inners)
        x = out[0]
        if not last:
            h, edge = out[1:]
            left.append(along(edge, 1))
    return x[None]


def solution(mesh):
    fine = Mesh(mesh.devices.reshape(8, 2, 2, 4, 2), DP + SEQ)
    placed = (P(DP, SEQ, None), P(), P(), P(), P(DP, None), P(), P(), P())
    return jax.shard_map(
        on_device, mesh=fine, in_specs=placed, out_specs=P(DP, SEQ, None), check_vma=False
    )
```

```python
import functools

import jax
import jax.numpy as jnp
from jax import lax
from jax.experimental import pallas as pl
from jax.experimental.pallas import tpu as pltpu
from jax.sharding import Mesh, PartitionSpec as P

HEAD = 64
KERNEL = 31
ITERS = 2
HALO = 16
EPS = 1e-05
DP = ("z", "yh")
SEQ = ("yl", "x", "core")
BF = jnp.bfloat16
F32 = jnp.float32
VMEM = 24 * 1024 * 1024


def params(**kw):
    return pltpu.CompilerParams(vmem_limit_bytes=VMEM, **kw)


def in_vmem(v):
    return pltpu.with_memory_space_constraint(v, pltpu.VMEM)


def in_hbm(v):
    return pltpu.with_memory_space_constraint(v, pltpu.HBM)


def normed(v):
    mean = jnp.mean(v, axis=-1, keepdims=True)
    d = v - mean
    var = jnp.mean(d * d, axis=-1, keepdims=True)
    return d * lax.rsqrt(var + EPS)


def pick_kernel(row_ref, in_ref, out_ref):
    for r in range(in_ref.shape[0]):
        out_ref[r] = in_ref[row_ref[r]]


def pick(chunks, row):
    return pl.pallas_call(
        pick_kernel,
        out_shape=jax.ShapeDtypeStruct(chunks.shape, chunks.dtype),
        in_specs=[
            pl.BlockSpec(memory_space=pltpu.SMEM),
            pl.BlockSpec(memory_space=pltpu.VMEM),
        ],
        out_specs=pl.BlockSpec(memory_space=pltpu.VMEM),
        compiler_params=params(),
        name="pick",
    )(row, chunks)


def head_kernel(x_ref, gain_ref, out_ref):
    out_ref[...] = (normed(x_ref[...].astype(F32)) * gain_ref[...]).astype(BF)


def head(x, gain):
    return pl.pallas_call(
        head_kernel,
        out_shape=jax.ShapeDtypeStruct(x.shape, BF),
        compiler_params=params(),
        name="head",
    )(x, gain)


def project_kernel(h_ref, w_ref, out_ref):
    for b in range(w_ref.shape[0]):
        out_ref[b] = jnp.dot(h_ref[...], w_ref[b], preferred_element_type=F32).astype(BF)


def project(h, w):
    blocks, _, cols = w.shape
    return pl.pallas_call(
        project_kernel,
        out_shape=pltpu.VMEM((blocks, h.shape[0], cols), BF),
        compiler_params=params(),
        name="project",
    )(h, in_vmem(w))


def heads(query, keys, values, bias):
    span = query.shape[0]
    lane = lax.broadcasted_iota(jnp.int32, (span, 128), 1)
    low = lane < HEAD
    tag = jnp.where(lane == 0, 1.0, 0.0).astype(BF)
    ones = jnp.ones((2 * span, 128), BF)
    outs = []
    for at in range(0, query.shape[1], 128):
        k = jnp.concatenate([keys[:, at : at + 128], bias], axis=1)
        v = jnp.concatenate([values[:, at : at + 128], ones], axis=1)
        q = query[:, at : at + 128] * jnp.asarray(HEAD ** (-0.5), BF)
        halves = []
        for mask in (low, jnp.logical_not(low)):
            qh = jnp.concatenate([jnp.where(mask, q, jnp.zeros_like(q)), tag], axis=1)
            s = lax.dot_general(qh, k, (((1,), (1,)), ((), ())), preferred_element_type=F32)
            top = jnp.max(s, axis=-1, keepdims=True)
            e = jnp.exp(s - top).astype(BF)
            o = jnp.dot(e, v, preferred_element_type=F32)
            halves.append(o[:, :128] / o[:, 128:])
        outs.append(jnp.where(low, halves[0], halves[1]).astype(BF))
    return jnp.concatenate(outs, axis=1)


def settle(ctx, fetch, wout_ref, x_ref, gain_ref, valid_ref, x1_ref, g_ref, ctx_ref):
    b = pl.program_id(0)
    group = ctx.shape[1]
    ctx_ref[:, pl.ds(pl.multiple_of(b * group, group), group)] = ctx

    @pl.when(b == pl.num_programs(0) - 1)
    def _():
        fetch.wait()
        x1 = x_ref[...].astype(F32) + jnp.dot(
            ctx_ref[...], wout_ref[...], preferred_element_type=F32
        )
        x1_ref[...] = x1
        g_ref[...] = (normed(x1) * gain_ref[...] * valid_ref[...]).astype(BF)


OFFSETS = (0, 3, 1, 2)


def opening_kernel(at_ref, h_ref, *refs):
    mine, other = refs[:8], refs[8:16]
    wall_ref, out_ref, sem = refs[16:]
    blocks = wall_ref.shape[0]
    half, rows = mine[0].shape[1:3]
    z, y, x, core = (at_ref[i] for i in range(4))

    def unit(held, j, u):
        return held[2 * j + u // 2].at[u % 2]

    def fetch(b):
        block = lax.rem(x + OFFSETS[b], blocks)
        for lane in range(2):
            for held, here in ((mine, core == lane), (other, core != lane)):

                @pl.when(here)
                def _():
                    for k in range(len(OFFSETS)):
                        source = unit(held, b, k) if lane else unit(held, k, b)
                        part = lax.rem(y + OFFSETS[k], len(OFFSETS))
                        for slot in range(half):
                            to = lax.rem(z + 2 * half - (lane * half + slot), 2 * half)
                            row = pl.multiple_of((to * len(OFFSETS) + part) * rows, rows)
                            pltpu.make_async_copy(
                                source.at[slot], wall_ref.at[block, pl.ds(row, rows)], sem.at[b]
                            ).start()

    for b in range(blocks):
        fetch(b)
    for b in range(blocks):
        block = lax.rem(x + OFFSETS[b], blocks)
        pltpu.make_async_copy(wall_ref.at[block], wall_ref.at[block], sem.at[b]).wait()
        out_ref[block] = jnp.dot(
            h_ref[...], wall_ref[block], preferred_element_type=F32
        ).astype(BF)


def opening(at, h, mine, other):
    _, half, rows, cols = mine[0].shape
    depth = 2 * half * len(OFFSETS) * rows
    blocks = len(OFFSETS)
    space = pl.BlockSpec(memory_space=pltpu.VMEM)
    anywhere = pl.BlockSpec(memory_space=pl.ANY)
    return pl.pallas_call(
        opening_kernel,
        out_shape=(
            pltpu.VMEM((blocks, depth, cols), BF),
            pltpu.VMEM((blocks, h.shape[0], cols), BF),
        ),
        in_specs=[pl.BlockSpec(memory_space=pltpu.SMEM), space] + [anywhere] * 16,
        out_specs=(space, space),
        scratch_shapes=[pltpu.SemaphoreType.DMA((blocks,))],
        compiler_params=params(),
        name="opening",
    )(at, h, *(in_hbm(v) for v in (*mine, *other)))


def whole(*shape):
    return pl.BlockSpec(shape, lambda b: (0,) * len(shape))


def attend_kernel(count, *refs):
    came = refs[:count]
    own_ref, w_ref, wout_ref, x_ref, bias_ref, gain_ref, valid_ref = refs[count : count + 7]
    x1_ref, g_ref, ctx_ref, left_ref, held_ref, sem = refs[count + 7 :]
    fetch = pltpu.make_async_copy(wout_ref, held_ref, sem)
    b = pl.program_id(0)
    group = wout_ref.shape[0] // w_ref.shape[0]
    span = left_ref.shape[0]

    @pl.when(b == 0)
    def _():
        fetch.start()
        if count == 1:
            left_ref[...] = came[0][...]
        else:
            inner_ref, edge_ref = came
            left_ref[pl.ds(0, HALO), :] = edge_ref[pl.ds(0, HALO), :]
            left_ref[pl.ds(HALO, span - 2 * HALO), :] = inner_ref[...]
            left_ref[pl.ds(span - HALO, HALO), :] = edge_ref[pl.ds(HALO, HALO), :]

    left = jnp.dot(left_ref[...], w_ref[b, :, : 2 * group], preferred_element_type=F32).astype(BF)
    own = own_ref[b]
    keys = jnp.concatenate([left[:, :group], own[:, :group]], axis=0)
    values = jnp.concatenate([left[:, group:], own[:, group : 2 * group]], axis=0)
    ctx = heads(own[:, 2 * group :], keys, values, bias_ref[...])
    settle(ctx, fetch, held_ref, x_ref, gain_ref, valid_ref, x1_ref, g_ref, ctx_ref)


def attend(left, own, w, w_out, x, bias, gain, valid):
    blocks = w.shape[0]
    span, width = x.shape
    group = width // blocks
    return pl.pallas_call(
        functools.partial(attend_kernel, len(left)),
        grid=(blocks,),
        out_shape=(
            jax.ShapeDtypeStruct((span, width), F32),
            jax.ShapeDtypeStruct((span, width), BF),
        ),
        in_specs=[
            *(whole(*v.shape) for v in left),
            pl.BlockSpec(memory_space=pltpu.VMEM),
            pl.BlockSpec(memory_space=pltpu.VMEM),
            pl.BlockSpec(memory_space=pl.ANY),
            whole(span, width),
            whole(2 * span, 128),
            whole(1, width),
            whole(span, 1),
        ],
        out_specs=(whole(span, width), whole(span, width)),
        scratch_shapes=[
            pltpu.VMEM((span, width), BF),
            pltpu.VMEM((span, width), BF),
            pltpu.VMEM((width, width), BF),
            pltpu.SemaphoreType.DMA(()),
        ],
        compiler_params=params(),
        name="attend",
    )(*left, in_vmem(own), in_vmem(w), in_hbm(w_out), x, bias, gain, valid)


def taps_over(pad_ref, taps, rows):
    y = jnp.zeros((rows, 128), F32)
    for r in range(8):
        hits = [(j, (j + 1) // 8) for j in range(KERNEL) if (j + 1) % 8 == r]
        deep = max(m for _, m in hits)
        moved = pad_ref[pl.ds(r, rows + 8 * deep), :]
        for j, m in hits:
            y = y + taps[j : j + 1, :] * moved[8 * m : 8 * m + rows]
    return y / (1.0 + jnp.exp(-y))


def inner_kernel(g_ref, x1_ref, taps_ref, valid_ref, gain_ref, x_ref, *rest):
    pad_ref = rest[-1]
    span, width = x1_ref.shape
    rows = pl.ds(HALO, span - 2 * HALO)
    for c in range(width // 128):
        cols = pl.ds(128 * c, 128)
        pad_ref[...] = g_ref[:, cols].astype(F32)
        silu = taps_over(pad_ref, taps_ref[:, cols], span - 2 * HALO)
        x_ref[:, cols] = ((x1_ref[rows, cols] + silu) * valid_ref[rows, :]).astype(BF)
    if len(rest) > 1:
        rest[0][...] = (normed(x_ref[...].astype(F32)) * gain_ref[...]).astype(BF)


def inner(g, x1, taps, valid, gain, last):
    span, width = x1.shape
    out = jax.ShapeDtypeStruct((span - 2 * HALO, width), BF)
    return pl.pallas_call(
        inner_kernel,
        out_shape=(out,) * (1 if last else 2),
        scratch_shapes=[pltpu.VMEM((span, 128), F32)],
        compiler_params=params(),
        name="inner",
    )(g, x1, taps, valid, gain)


def edges_kernel(count, g_ref, low_ref, high_ref, x1_ref, taps_ref, valid_ref, gain_ref, *rest):
    ins, outs, pad_ref = rest[:count], rest[count:-1], rest[-1]
    if count > 1:
        outs, edge_ref = outs[:-1], outs[-1]
    span, width = x1_ref.shape
    x_ref = outs[0]
    for at in (0, span - HALO):
        rows = pl.ds(at, HALO)
        for c in range(width // 128):
            cols = pl.ds(128 * c, 128)
            if at == 0:
                pad_ref[pl.ds(0, HALO), :] = low_ref[:, cols].astype(F32)
                pad_ref[pl.ds(HALO, 2 * HALO), :] = g_ref[pl.ds(0, 2 * HALO), cols].astype(F32)
            else:
                pad_ref[pl.ds(0, 2 * HALO), :] = g_ref[pl.ds(span - 2 * HALO, 2 * HALO), cols].astype(F32)
                pad_ref[pl.ds(2 * HALO, HALO), :] = high_ref[:, cols].astype(F32)
            silu = taps_over(pad_ref, taps_ref[:, cols], HALO)
            x_ref[rows, cols] = ((x1_ref[rows, cols] + silu) * valid_ref[rows, :]).astype(BF)
        if count > 1:
            h = (normed(x_ref[rows, :].astype(F32)) * gain_ref[...]).astype(BF)
            outs[1][rows, :] = h
            edge_ref[pl.ds(HALO if at else 0, HALO), :] = h
    rows = pl.ds(HALO, span - 2 * HALO)
    for source, target in zip(ins, outs):
        target[rows, :] = source[...]


def edges(g, low, high, x1, taps, valid, gain, inners):
    span, width = x1.shape
    count = len(inners)
    return pl.pallas_call(
        functools.partial(edges_kernel, count),
        out_shape=(jax.ShapeDtypeStruct((span, width), BF),) * count
        + (jax.ShapeDtypeStruct((2 * HALO, width), BF),) * (count - 1),
        scratch_shapes=[pltpu.VMEM((3 * HALO, 128), F32)],
        compiler_params=params(),
        name="edges",
    )(g, low, high, x1, taps, valid, gain, *inners)


def along(value, by):
    size = lax.axis_size(SEQ)
    pairs = [(i, i + by) for i in range(size) if 0 <= i + by < size]
    return lax.ppermute(value, SEQ, pairs)


def around(value, phase, by):
    ys = lax.axis_size("yh") * lax.axis_size("yl")
    xs, cores = lax.axis_size("x"), lax.axis_size("core")
    at = lambda y, x, core: ((y % ys) * xs + x % xs) * cores + core
    pairs = []
    for y in range(ys):
        for x in range(xs):
            for core in range(cores):
                along_x = (core == 0) == (phase == 1)
                to = at(y, x + by, core) if along_x else at(y + by, x, core)
                pairs.append((at(y, x, core), to))
    return lax.ppermute(value, ("yh", "yl", "x", "core"), pairs)


def weight_row(w):
    rows, cols = w.shape
    zs, xs, yls, cores = (lax.axis_size(a) for a in ("z", "x", "yl", "core"))
    deep = rows // yls
    width = cols // 3
    group = width // xs
    at = lax.axis_index("yl") * deep
    col = lax.axis_index("x") * group
    own = jnp.concatenate(
        [lax.dynamic_slice(w, (at, part * width + col), (deep, group)) for part in (1, 2, 0)],
        axis=1,
    )
    half = zs // cores
    came = {}
    for k in range(1, half + 1):
        pairs = [(cores * z, cores * ((z + k) % zs)) for z in range(zs) if k < half]
        pairs += [(cores * z + 1, cores * ((z - k) % zs) + 1) for z in range(zs)]
        came[k] = lax.ppermute(own, ("z", "core"), pairs)
    first = lax.axis_index("core") == 0
    stack = jnp.concatenate(
        [
            jnp.where(first, came[k] if k else own, came[half - k])
            for k in range(half)
        ],
        axis=0,
    )
    unit = stack.reshape(half, deep, 3 * group)
    before, after = around(unit, 1, 1), around(unit, 1, -1)
    far = [around(before[: half // 2], 1, 1), around(after[half // 2 :], 1, -1)]
    front = jnp.stack([unit, before])
    back = jnp.stack([after, jnp.concatenate(far, axis=0)])
    return front, back


def swapped(values):
    return [lax.ppermute(v, "core", [(0, 1), (1, 0)]) for v in values]


def on_device(frames, arrival, lengths, attn_gain, w_qkv, w_out, conv_gain, conv_kernel):
    span = frames.shape[1]
    width = w_out.shape[0]
    group = lax.axis_index(DP)
    place = lax.axis_index(SEQ)
    groups = lax.axis_size(DP)
    front, back = weight_row(w_qkv)
    row_here = lax.dynamic_index_in_dim(arrival, place, 0, keepdims=False)
    chunks = frames.reshape(groups, span // groups, width)
    chunks = lax.all_to_all(chunks, DP, split_axis=0, concat_axis=0, tiled=True)
    chunks, front, back = lax.optimization_barrier((chunks, front, back))
    before = [around(front, 2, 1), around(back, 2, 1)]
    after = [around(front, 2, -1), around(back, 2, -1)]
    chunks = pick(chunks, row_here)
    chunks = lax.all_to_all(chunks, DP, split_axis=0, concat_axis=0, tiled=True)
    far = [around(before[0], 2, 1), around(after[1], 2, -1)]
    x = chunks.reshape(span, width)
    mine = [front, back] + before + after + far
    other = swapped(mine)

    length = lax.dynamic_index_in_dim(lengths, group, 0, keepdims=False)
    position = place * span + jnp.arange(span)
    own_valid = position < length
    left_valid = jnp.logical_and(position - span < length, place > 0)
    key_valid = jnp.concatenate([left_valid, own_valid])
    bias = jnp.where(key_valid, 0.0, -1e30).astype(BF)
    bias = jnp.where(jnp.arange(128)[None, :] == 0, bias[:, None], jnp.zeros((), BF))
    valid = own_valid.astype(F32)[:, None]
    gain_a = attn_gain[None, :]
    gain_c = conv_gain[None, :]
    taps = jnp.pad(conv_kernel, ((0, 1), (0, 0)))

    h = head(x, gain_a)
    left = [along(h, 1)]
    for step in range(ITERS):
        last = step == ITERS - 1
        if step == 0:
            at = [lax.axis_index(a) for a in ("z", ("yh", "yl"), "x", "core")]
            w, own = opening(jnp.stack(at).astype(jnp.int32), h, mine, other)
        else:
            own = project(h, w)
        x1, g = attend(left, own, w, w_out, x, bias, gain_c, valid)
        low = along(g[span - HALO :], 1)
        high = along(g[:HALO], -1)
        inners = inner(g, x1, taps, valid, gain_a, last)
        if not last:
            h_inner, low = lax.optimization_barrier((inners[1], low))
            inners = (inners[0], h_inner)
            left = [along(h_inner, 1)]
        out = edges(g, low, high, x1, taps, valid, gain_a, inners)
        x = out[0]
        if not last:
            h, edge = out[1:]
            left.append(along(edge, 1))
    return x[None]


def solution(mesh):
    fine = Mesh(mesh.devices.reshape(8, 2, 2, 4, 2), DP + SEQ)
    placed = (P(DP, SEQ, None), P(), P(), P(), P(DP, None), P(), P(), P())
    return jax.shard_map(
        on_device, mesh=fine, in_specs=placed, out_specs=P(DP, SEQ, None), check_vma=False
    )
```

```python
import functools

import jax
import jax.numpy as jnp
from jax import lax
from jax.experimental import pallas as pl
from jax.experimental.pallas import tpu as pltpu
from jax.sharding import Mesh, PartitionSpec as P

HEAD = 64
KERNEL = 31
ITERS = 2
HALO = 16
EPS = 1e-05
DP = ("z", "yh")
SEQ = ("yl", "x", "core")
BF = jnp.bfloat16
F32 = jnp.float32
VMEM = 24 * 1024 * 1024


def params(**kw):
    return pltpu.CompilerParams(vmem_limit_bytes=VMEM, **kw)


def in_vmem(v):
    return pltpu.with_memory_space_constraint(v, pltpu.VMEM)


def in_hbm(v):
    return pltpu.with_memory_space_constraint(v, pltpu.HBM)


def normed(v):
    mean = jnp.mean(v, axis=-1, keepdims=True)
    d = v - mean
    var = jnp.mean(d * d, axis=-1, keepdims=True)
    return d * lax.rsqrt(var + EPS)


def pick_kernel(row_ref, in_ref, out_ref):
    for r in range(in_ref.shape[0]):
        out_ref[r] = in_ref[row_ref[r]]


def pick(chunks, row):
    return pl.pallas_call(
        pick_kernel,
        out_shape=jax.ShapeDtypeStruct(chunks.shape, chunks.dtype),
        in_specs=[
            pl.BlockSpec(memory_space=pltpu.SMEM),
            pl.BlockSpec(memory_space=pltpu.VMEM),
        ],
        out_specs=pl.BlockSpec(memory_space=pltpu.VMEM),
        compiler_params=params(),
        name="pick",
    )(row, chunks)


def head_kernel(x_ref, gain_ref, out_ref):
    out_ref[...] = (normed(x_ref[...].astype(F32)) * gain_ref[...]).astype(BF)


def head(x, gain):
    return pl.pallas_call(
        head_kernel,
        out_shape=jax.ShapeDtypeStruct(x.shape, BF),
        compiler_params=params(),
        name="head",
    )(x, gain)


def project_kernel(h_ref, w_ref, out_ref):
    for b in range(w_ref.shape[0]):
        out_ref[b] = jnp.dot(h_ref[...], w_ref[b], preferred_element_type=F32).astype(BF)


def project(h, w):
    blocks, _, cols = w.shape
    return pl.pallas_call(
        project_kernel,
        out_shape=pltpu.VMEM((blocks, h.shape[0], cols), BF),
        compiler_params=params(),
        name="project",
    )(h, in_vmem(w))


def heads(query, keys, values, bias):
    span = query.shape[0]
    lane = lax.broadcasted_iota(jnp.int32, (span, 128), 1)
    low = lane < HEAD
    tag = jnp.where(lane == 0, 1.0, 0.0).astype(BF)
    ones = jnp.ones((2 * span, 128), BF)
    outs = []
    for at in range(0, query.shape[1], 128):
        k = jnp.concatenate([keys[:, at : at + 128], bias], axis=1)
        v = jnp.concatenate([values[:, at : at + 128], ones], axis=1)
        q = query[:, at : at + 128] * jnp.asarray(HEAD ** (-0.5), BF)
        halves = []
        for mask in (low, jnp.logical_not(low)):
            qh = jnp.concatenate([jnp.where(mask, q, jnp.zeros_like(q)), tag], axis=1)
            s = lax.dot_general(qh, k, (((1,), (1,)), ((), ())), preferred_element_type=F32)
            top = jnp.max(s, axis=-1, keepdims=True)
            e = jnp.exp(s - top).astype(BF)
            o = jnp.dot(e, v, preferred_element_type=F32)
            halves.append(o[:, :128] / o[:, 128:])
        outs.append(jnp.where(low, halves[0], halves[1]).astype(BF))
    return jnp.concatenate(outs, axis=1)


def settle(ctx, fetch, wout_ref, x_ref, gain_ref, valid_ref, x1_ref, g_ref, ctx_ref):
    b = pl.program_id(0)
    group = ctx.shape[1]
    ctx_ref[:, pl.ds(pl.multiple_of(b * group, group), group)] = ctx

    @pl.when(b == pl.num_programs(0) - 1)
    def _():
        fetch.wait()
        x1 = x_ref[...].astype(F32) + jnp.dot(
            ctx_ref[...], wout_ref[...], preferred_element_type=F32
        )
        x1_ref[...] = x1
        g_ref[...] = (normed(x1) * gain_ref[...] * valid_ref[...]).astype(BF)


OFFSETS = (0, 3, 1, 2)


def opening_kernel(at_ref, h_ref, *refs):
    mine, other = refs[:8], refs[8:16]
    wall_ref, out_ref, sem = refs[16:]
    blocks = wall_ref.shape[0]
    half, rows = mine[0].shape[1:3]
    z, y, x, core = (at_ref[i] for i in range(4))

    def unit(held, j, u):
        return held[2 * j + u // 2].at[u % 2]

    def fetch(b):
        block = lax.rem(x + OFFSETS[b], blocks)
        for lane in range(2):
            for held, here in ((mine, core == lane), (other, core != lane)):

                @pl.when(here)
                def _():
                    for k in range(len(OFFSETS)):
                        source = unit(held, b, k) if lane else unit(held, k, b)
                        part = lax.rem(y + OFFSETS[k], len(OFFSETS))
                        for slot in range(half):
                            to = lax.rem(z + 2 * half - (lane * half + slot), 2 * half)
                            row = pl.multiple_of((to * len(OFFSETS) + part) * rows, rows)
                            pltpu.make_async_copy(
                                source.at[slot], wall_ref.at[block, pl.ds(row, rows)], sem.at[b]
                            ).start()

    for b in range(blocks):
        fetch(b)
    for b in range(blocks):
        block = lax.rem(x + OFFSETS[b], blocks)
        pltpu.make_async_copy(wall_ref.at[block], wall_ref.at[block], sem.at[b]).wait()
        out_ref[block] = jnp.dot(
            h_ref[...], wall_ref[block], preferred_element_type=F32
        ).astype(BF)


def opening(at, h, mine, other):
    _, half, rows, cols = mine[0].shape
    depth = 2 * half * len(OFFSETS) * rows
    blocks = len(OFFSETS)
    space = pl.BlockSpec(memory_space=pltpu.VMEM)
    anywhere = pl.BlockSpec(memory_space=pl.ANY)
    return pl.pallas_call(
        opening_kernel,
        out_shape=(
            pltpu.VMEM((blocks, depth, cols), BF),
            pltpu.VMEM((blocks, h.shape[0], cols), BF),
        ),
        in_specs=[pl.BlockSpec(memory_space=pltpu.SMEM), space] + [anywhere] * 16,
        out_specs=(space, space),
        scratch_shapes=[pltpu.SemaphoreType.DMA((blocks,))],
        compiler_params=params(),
        name="opening",
    )(at, h, *(in_hbm(v) for v in (*mine, *other)))


def whole(*shape):
    return pl.BlockSpec(shape, lambda b: (0,) * len(shape))


def attend_kernel(count, *refs):
    came = refs[:count]
    own_ref, w_ref, wout_ref, x_ref, bias_ref, gain_ref, valid_ref = refs[count : count + 7]
    x1_ref, g_ref, ctx_ref, left_ref, held_ref, sem = refs[count + 7 :]
    fetch = pltpu.make_async_copy(wout_ref, held_ref, sem)
    b = pl.program_id(0)
    group = wout_ref.shape[0] // w_ref.shape[0]
    span = left_ref.shape[0]

    @pl.when(b == 0)
    def _():
        fetch.start()
        if count == 1:
            left_ref[...] = came[0][...]
        else:
            inner_ref, edge_ref = came
            left_ref[pl.ds(0, HALO), :] = edge_ref[pl.ds(0, HALO), :]
            left_ref[pl.ds(HALO, span - 2 * HALO), :] = inner_ref[...]
            left_ref[pl.ds(span - HALO, HALO), :] = edge_ref[pl.ds(HALO, HALO), :]

    left = jnp.dot(left_ref[...], w_ref[b, :, : 2 * group], preferred_element_type=F32).astype(BF)
    own = own_ref[b]
    keys = jnp.concatenate([left[:, :group], own[:, :group]], axis=0)
    values = jnp.concatenate([left[:, group:], own[:, group : 2 * group]], axis=0)
    ctx = heads(own[:, 2 * group :], keys, values, bias_ref[...])
    settle(ctx, fetch, held_ref, x_ref, gain_ref, valid_ref, x1_ref, g_ref, ctx_ref)


def attend(left, own, w, w_out, x, bias, gain, valid):
    blocks = w.shape[0]
    span, width = x.shape
    group = width // blocks
    return pl.pallas_call(
        functools.partial(attend_kernel, len(left)),
        grid=(blocks,),
        out_shape=(
            jax.ShapeDtypeStruct((span, width), F32),
            jax.ShapeDtypeStruct((span, width), BF),
        ),
        in_specs=[
            *(whole(*v.shape) for v in left),
            pl.BlockSpec(memory_space=pltpu.VMEM),
            pl.BlockSpec(memory_space=pltpu.VMEM),
            pl.BlockSpec(memory_space=pl.ANY),
            whole(span, width),
            whole(2 * span, 128),
            whole(1, width),
            whole(span, 1),
        ],
        out_specs=(whole(span, width), whole(span, width)),
        scratch_shapes=[
            pltpu.VMEM((span, width), BF),
            pltpu.VMEM((span, width), BF),
            pltpu.VMEM((width, width), BF),
            pltpu.SemaphoreType.DMA(()),
        ],
        compiler_params=params(),
        name="attend",
    )(*left, in_vmem(own), in_vmem(w), in_hbm(w_out), x, bias, gain, valid)


def taps_over(pad_ref, taps, rows):
    y = jnp.zeros((rows, 128), F32)
    for r in range(8):
        hits = [(j, (j + 1) // 8) for j in range(KERNEL) if (j + 1) % 8 == r]
        deep = max(m for _, m in hits)
        moved = pad_ref[pl.ds(r, rows + 8 * deep), :]
        for j, m in hits:
            y = y + taps[j : j + 1, :] * moved[8 * m : 8 * m + rows]
    return y / (1.0 + jnp.exp(-y))


def inner_kernel(g_ref, x1_ref, taps_ref, valid_ref, gain_ref, x_ref, *rest):
    pad_ref = rest[-1]
    span, width = x1_ref.shape
    rows = pl.ds(HALO, span - 2 * HALO)
    for c in range(width // 128):
        cols = pl.ds(128 * c, 128)
        pad_ref[...] = g_ref[:, cols].astype(F32)
        silu = taps_over(pad_ref, taps_ref[:, cols], span - 2 * HALO)
        x_ref[:, cols] = ((x1_ref[rows, cols] + silu) * valid_ref[rows, :]).astype(BF)
    if len(rest) > 1:
        rest[0][...] = (normed(x_ref[...].astype(F32)) * gain_ref[...]).astype(BF)


def inner(g, x1, taps, valid, gain, last):
    span, width = x1.shape
    out = jax.ShapeDtypeStruct((span - 2 * HALO, width), BF)
    return pl.pallas_call(
        inner_kernel,
        out_shape=(out,) * (1 if last else 2),
        scratch_shapes=[pltpu.VMEM((span, 128), F32)],
        compiler_params=params(),
        name="inner",
    )(g, x1, taps, valid, gain)


def edges_kernel(count, core_ref, g_ref, inside_ref, outside_ref, x1_ref, taps_ref, valid_ref, gain_ref, *rest):
    ins, outs, pad_ref = rest[:count], rest[count:-1], rest[-1]
    if count > 1:
        outs, edge_ref = outs[:-1], outs[-1]
    span, width = x1_ref.shape
    x_ref = outs[0]
    first = core_ref[0] == 0
    for at in (0, span - HALO):
        rows = pl.ds(at, HALO)
        for c in range(width // 128):
            cols = pl.ds(128 * c, 128)
            if at == 0:
                low = jnp.where(first, outside_ref[:, cols], inside_ref[:, cols])
                pad_ref[pl.ds(0, HALO), :] = low.astype(F32)
                pad_ref[pl.ds(HALO, 2 * HALO), :] = g_ref[pl.ds(0, 2 * HALO), cols].astype(F32)
            else:
                pad_ref[pl.ds(0, 2 * HALO), :] = g_ref[pl.ds(span - 2 * HALO, 2 * HALO), cols].astype(F32)
                high = jnp.where(first, inside_ref[:, cols], outside_ref[:, cols])
                pad_ref[pl.ds(2 * HALO, HALO), :] = high.astype(F32)
            silu = taps_over(pad_ref, taps_ref[:, cols], HALO)
            x_ref[rows, cols] = ((x1_ref[rows, cols] + silu) * valid_ref[rows, :]).astype(BF)
        if count > 1:
            h = (normed(x_ref[rows, :].astype(F32)) * gain_ref[...]).astype(BF)
            outs[1][rows, :] = h
            edge_ref[pl.ds(HALO if at else 0, HALO), :] = h
    rows = pl.ds(HALO, span - 2 * HALO)
    for source, target in zip(ins, outs):
        target[rows, :] = source[...]


def edges(core, g, inside, outside, x1, taps, valid, gain, inners):
    span, width = x1.shape
    count = len(inners)
    return pl.pallas_call(
        functools.partial(edges_kernel, count),
        in_specs=[pl.BlockSpec(memory_space=pltpu.SMEM)]
        + [pl.BlockSpec(memory_space=pltpu.VMEM)] * (7 + count),
        out_shape=(jax.ShapeDtypeStruct((span, width), BF),) * count
        + (jax.ShapeDtypeStruct((2 * HALO, width), BF),) * (count - 1),
        scratch_shapes=[pltpu.VMEM((3 * HALO, 128), F32)],
        compiler_params=params(),
        name="edges",
    )(core, g, inside, outside, x1, taps, valid, gain, *inners)


def along(value, by):
    size = lax.axis_size(SEQ)
    pairs = [(i, i + by) for i in range(size) if 0 <= i + by < size]
    return lax.ppermute(value, SEQ, pairs)


def around(value, phase, by):
    ys = lax.axis_size("yh") * lax.axis_size("yl")
    xs, cores = lax.axis_size("x"), lax.axis_size("core")
    at = lambda y, x, core: ((y % ys) * xs + x % xs) * cores + core
    pairs = []
    for y in range(ys):
        for x in range(xs):
            for core in range(cores):
                along_x = (core == 0) == (phase == 1)
                to = at(y, x + by, core) if along_x else at(y + by, x, core)
                pairs.append((at(y, x, core), to))
    return lax.ppermute(value, ("yh", "yl", "x", "core"), pairs)


def weight_row(w):
    rows, cols = w.shape
    zs, xs, yls, cores = (lax.axis_size(a) for a in ("z", "x", "yl", "core"))
    deep = rows // yls
    width = cols // 3
    group = width // xs
    at = lax.axis_index("yl") * deep
    col = lax.axis_index("x") * group
    own = jnp.concatenate(
        [lax.dynamic_slice(w, (at, part * width + col), (deep, group)) for part in (1, 2, 0)],
        axis=1,
    )
    half = zs // cores
    came = {}
    for k in range(1, half + 1):
        pairs = [(cores * z, cores * ((z + k) % zs)) for z in range(zs) if k < half]
        pairs += [(cores * z + 1, cores * ((z - k) % zs) + 1) for z in range(zs)]
        came[k] = lax.ppermute(own, ("z", "core"), pairs)
    first = lax.axis_index("core") == 0
    stack = jnp.concatenate(
        [
            jnp.where(first, came[k] if k else own, came[half - k])
            for k in range(half)
        ],
        axis=0,
    )
    unit = stack.reshape(half, deep, 3 * group)
    before, after = around(unit, 1, 1), around(unit, 1, -1)
    far = [around(before[: half // 2], 1, 1), around(after[half // 2 :], 1, -1)]
    front = jnp.stack([unit, before])
    back = jnp.stack([after, jnp.concatenate(far, axis=0)])
    return front, back


def across(value):
    size = lax.axis_size(SEQ)
    pairs = [(i, i + 1) for i in range(1, size - 1, 2)]
    return lax.ppermute(value, SEQ, pairs + [(b, a) for a, b in pairs])


def swapped(values):
    return [lax.ppermute(v, "core", [(0, 1), (1, 0)]) for v in values]


def on_device(frames, arrival, lengths, attn_gain, w_qkv, w_out, conv_gain, conv_kernel):
    span = frames.shape[1]
    width = w_out.shape[0]
    group = lax.axis_index(DP)
    place = lax.axis_index(SEQ)
    groups = lax.axis_size(DP)
    front, back = weight_row(w_qkv)
    row_here = lax.dynamic_index_in_dim(arrival, place, 0, keepdims=False)
    chunks = frames.reshape(groups, span // groups, width)
    chunks = lax.all_to_all(chunks, DP, split_axis=0, concat_axis=0, tiled=True)
    chunks, front, back = lax.optimization_barrier((chunks, front, back))
    before = [around(front, 2, 1), around(back, 2, 1)]
    after = [around(front, 2, -1), around(back, 2, -1)]
    chunks = pick(chunks, row_here)
    chunks = lax.all_to_all(chunks, DP, split_axis=0, concat_axis=0, tiled=True)
    far = [around(before[0], 2, 1), around(after[1], 2, -1)]
    x = chunks.reshape(span, width)
    mine = [front, back] + before + after + far
    other = swapped(mine)

    length = lax.dynamic_index_in_dim(lengths, group, 0, keepdims=False)
    position = place * span + jnp.arange(span)
    own_valid = position < length
    left_valid = jnp.logical_and(position - span < length, place > 0)
    key_valid = jnp.concatenate([left_valid, own_valid])
    bias = jnp.where(key_valid, 0.0, -1e30).astype(BF)
    bias = jnp.where(jnp.arange(128)[None, :] == 0, bias[:, None], jnp.zeros((), BF))
    valid = own_valid.astype(F32)[:, None]
    gain_a = attn_gain[None, :]
    gain_c = conv_gain[None, :]
    taps = jnp.pad(conv_kernel, ((0, 1), (0, 0)))

    h = head(x, gain_a)
    left = [along(h, 1)]
    for step in range(ITERS):
        last = step == ITERS - 1
        if step == 0:
            at = [lax.axis_index(a) for a in ("z", ("yh", "yl"), "x", "core")]
            w, own = opening(jnp.stack(at).astype(jnp.int32), h, mine, other)
        else:
            own = project(h, w)
        x1, g = attend(left, own, w, w_out, x, bias, gain_c, valid)
        first = lax.axis_index("core") == 0
        inside = swapped([jnp.where(first, g[span - HALO :], g[:HALO])])[0]
        outside = across(jnp.where(first, g[:HALO], g[span - HALO :]))
        inners = inner(g, x1, taps, valid, gain_a, last)
        if not last:
            h_inner, inside, outside = lax.optimization_barrier((inners[1], inside, outside))
            inners = (inners[0], h_inner)
            left = [along(h_inner, 1)]
        core = lax.axis_index("core").astype(jnp.int32)[None]
        out = edges(core, g, inside, outside, x1, taps, valid, gain_a, inners)
        x = out[0]
        if not last:
            h, edge = out[1:]
            left.append(along(edge, 1))
    return x[None]


def solution(mesh):
    fine = Mesh(mesh.devices.reshape(8, 2, 2, 4, 2), DP + SEQ)
    placed = (P(DP, SEQ, None), P(), P(), P(), P(DP, None), P(), P(), P())
    return jax.shard_map(
        on_device, mesh=fine, in_specs=placed, out_specs=P(DP, SEQ, None), check_vma=False
    )
```
